512 devices in a mesh: dp: 16 (over z, core), expert: 32 (over y, x).
Axes of the slice: x: 4, y: 8, z: 8, core: 2. Of those that a mesh axis runs over, the one named last changes fastest.
Arguments:
- tokens: bfloat16 [65536, 2048], P(('dp', 'expert')), may hold values from -6 to 6
- grad_out: bfloat16 [65536, 2048], P(('dp', 'expert')), may hold values from -6 to 6
- routes: int32 [65536, 4], P(('dp', 'expert')), may hold values from 0 to 47, all different within a row; in each aligned block of 128 rows (0 to 127, 128 to 255, ...) at most 13 rows name the same one
- gates: bfloat16 [65536, 4], P(('dp', 'expert')), may hold values from 0.099609375 to 1
- expert_tiles: int32 [48], replicated, may hold values from 1 to 4, 64 in all
- w_in: bfloat16 [64, 2048, 256], P('expert', 'dp'), may hold values from -0.125 to 0.125
- w_out: bfloat16 [64, 256, 2048], P('expert', None, 'dp'), may hold values from -0.25 to 0.25
Outputs:
- grad_tokens: bfloat16 [65536, 2048], P(('dp', 'expert'))
- grad_gates: float32 [65536, 4], P(('dp', 'expert'))
- grad_w_in: float32 [64, 2048, 256], P('expert', 'dp')
- grad_w_out: float32 [64, 256, 2048], P('expert', None, 'dp')
The draws below stay inside these ranges and needn't reach their ends.
Inputs may be any that keep to these rules, and one draw needn't show every extreme that they name: `routes`: among the rows of one device no expert is named by more than 13 rows, a bound that some block reaches; a row names 4 different experts and every expert is named somewhere. `expert_tiles`: the entries sum to 64 and the largest is 4.
All inputs are finite; a program needn't handle non-finite values.
Results may differ from the reference program's by a relative error of at most 0.02.
Values may be sent and summed in bfloat16 or wider, within the bound.
A program may use at most 64 MiB of HBM per device.

```python
import math
import jax
import jax.numpy as jnp
import numpy as np
from jax import lax

D = 2048
TILE = 256
TOP = 4
MAXT = 4
TOK_DEV = 128
EXPERTS = 48
TILES = 64
MOST = 13
TOKENS = 65536
N_DP = 16
N_EXPERT = 32


def block_scale(own_key, shape, split, least, high):
    def one(dim, blocks):
        heights = jax.random.uniform(jax.random.fold_in(jax.random.fold_in(own_key, 6), dim), (blocks,), jnp.float32, least / len(split), high / len(split))
        return jnp.repeat(jnp.exp(heights), shape[dim] // blocks).reshape((-1,) + (1,) * (len(shape) - dim - 1))

    level = one(*split[0])
    for cut in split[1:]:
        level = level * one(*cut)
    return level


def length_profile(count, total, bound, slope):
    weights = [(1 << 20) // math.isqrt(rank ** slope) + 1 for rank in range(2, count + 1)]
    rest, holding = total - bound - (count - 1), [1] * (count - 1)
    while rest > 0:
        movable = [i for i in range(count - 1) if holding[i] < bound]
        mass, left = sum([weights[i] for i in movable]), rest
        for i in movable:
            extra = min(bound - holding[i], max(1, left * weights[i] // mass), rest)
            holding[i] = holding[i] + extra
            rest = rest - extra
    return np.array([bound] + holding)


def ragged(key, amount, total, limit, slope):
    if amount == 2:
        one = jax.random.randint(key, (), max(1, total - limit), min(limit, total - 1) + 1)
        return jnp.stack([one, total - one])
    lengths = jnp.asarray(length_profile(amount, total, limit, slope), jnp.int32)
    twos = (amount - 1) // 2
    giver, sink = lengths[1:1 + 2 * twos:2], lengths[2:2 + 2 * twos:2]
    slack = jnp.minimum(giver - 1, limit - sink)
    passed = jax.random.randint(jax.random.fold_in(key, 1), (twos,), 0, 1 << 20) % (slack + 1)
    lengths = lengths.at[1:1 + 2 * twos:2].set(giver - passed).at[2:2 + 2 * twos:2].set(sink + passed)
    return lengths[jax.random.permutation(jax.random.fold_in(key, 2), amount)]


def routed_block(key, own, number, rows, count, top, limit, lean):
    order = jax.random.permutation(key, count)
    crowded, usual = load_shares(count, rows * top, limit, lean, True), load_shares(count, rows * top, limit, lean, False)
    places = jnp.arange(count)

    def named(sizes, rotation):
        used = int((sizes > 0).sum())
        fixed = max(1, used // 4)
        moved = fixed + (places - fixed + rotation * (used - fixed)) % max(1, count - fixed)
        return jnp.zeros((count,), jnp.int32).at[order[jnp.where(places < fixed, places, moved)]].set(jnp.asarray(sizes, jnp.int32))

    sizes = jnp.where(number % 4 == 0, named(crowded, number // 4), named(usual, number - number // 4 - 1))
    mixed = jax.random.permutation(jax.random.fold_in(own, 3), count)
    donor, sink = mixed[0:count // 2 * 2:2], mixed[1:count // 2 * 2:2]
    slack = jnp.minimum(sizes[donor] - 1, limit - sizes[sink]) // 2
    slack = jnp.where((donor == order[0]) | (sink == order[0]) | (sizes[sink] == 0), 0, jnp.maximum(slack, 0))
    moved = jax.random.randint(jax.random.fold_in(own, 4), (count // 2,), 0, 1 << 20) % (slack + 1)
    sizes = sizes.at[donor].add(-moved).at[sink].add(moved)
    labels = jnp.searchsorted(jnp.cumsum(sizes), jnp.arange(rows * top), side="right").astype(jnp.int32)
    table = labels.reshape(top, rows).T
    table = table[jax.random.permutation(jax.random.fold_in(own, 1), rows)]
    rotation = jax.random.randint(jax.random.fold_in(own, 2), (rows, 1), 0, top)
    return jnp.take_along_axis(table, (jnp.arange(top)[None, :] + rotation) % top, axis=1)


def load_shares(number_of, total, limit, skew, full):
    weights = [(1 << 20) // math.isqrt(rank ** skew) + 1 for rank in range(1, number_of + 1)]
    largest = limit if full else min(limit, max(-(-total // number_of), total * weights[0] // sum(weights)))
    least = 1 if total - largest >= number_of - 1 else 0
    counts, surplus = [largest] + [least] * (number_of - 1), total - largest - least * (number_of - 1)
    while surplus > 0:
        free = [i for i in range(1, number_of) if counts[i] < largest] or [i for i in range(1, number_of) if counts[i] < limit]
        whole, left = sum([weights[i] for i in free]), surplus
        for i in free:
            addition = min(limit - counts[i], max(1, left * weights[i] // whole), surplus)
            counts[i] = counts[i] + addition
            surplus = surplus - addition
    return np.array(counts)


def centred(own_key, extent, width, limit, split=(), kind=jnp.bfloat16):
    drawn = jax.random.normal(own_key, extent, jnp.float32) * width
    if len(split) > 0:
        drawn = block_scale(own_key, extent, split, -0.22, 0.18) * drawn
    return jnp.clip(drawn, min=-limit, max=limit).astype(kind)


def setup_inputs(seed: int = 0) -> dict:
    streams_of = jax.random.split(jax.random.key(seed), 8)
    tokens = centred(streams_of[0], (TOKENS, D), 1.0, 6.0, ((0, 512),))
    grad_out = centred(streams_of[1], (TOKENS, D), 1.0, 6.0, ((0, 512),))
    routes_keys = jax.random.split(jax.random.fold_in(streams_of[2], 1), TOKENS // TOK_DEV)
    routes_turns = jax.random.permutation(jax.random.fold_in(streams_of[2], 3), TOKENS // TOK_DEV)
    routes = jax.vmap(lambda own, number: routed_block(jax.random.fold_in(streams_of[2], 2), own, number, TOK_DEV, EXPERTS, TOP, MOST, 2))(routes_keys, routes_turns).reshape((TOKENS, TOP))
    gates = jnp.clip(0.099609375 + 0.9003906 * jax.random.uniform(streams_of[3], (TOKENS, TOP), jnp.float32) ** block_scale(streams_of[3], (TOKENS, TOP), ((0, 512),), -0.2, 0.2), 0.099609375, 1.0).astype(jnp.bfloat16)
    expert_tiles = ragged(streams_of[4], EXPERTS, TILES, MAXT, 1).astype(jnp.int32)
    w_in = centred(streams_of[5], (TILES, D, TILE), D ** -0.5, 0.125, ((0, 32), (1, 16)))
    w_out = centred(streams_of[6], (TILES, TILE, D), (2 * TILE) ** -0.5, 0.25, ((0, 32), (2, 16)))
    return {"tokens": tokens, "grad_out": grad_out, "routes": routes, "gates": gates, "expert_tiles": expert_tiles, "w_in": w_in, "w_out": w_out}


def gelu_pair(values):
    return jax.jvp(lambda inner: jax.nn.gelu(inner, approximate=True), (values,), (jnp.ones_like(values),))


def reference(tokens, grad_out, routes, gates, expert_tiles, w_in, w_out):
    expert_ids = routes.reshape(-1).astype(jnp.int32)
    gate_flat = gates.reshape(-1)
    assign_total = TOKENS * TOP
    block_assign = TOK_DEV * N_EXPERT * TOP
    block_of = (jnp.arange(assign_total, dtype=jnp.int32) // block_assign).astype(jnp.int32)
    sorted_ids = jnp.argsort(expert_ids, stable=True).astype(jnp.int32)
    pair_counts = jax.ops.segment_sum(jnp.ones((assign_total,), jnp.int32), expert_ids * N_DP + block_of, num_segments=EXPERTS * N_DP).astype(jnp.int32)
    pair_starts = (jnp.cumsum(pair_counts) - pair_counts).astype(jnp.int32).reshape(EXPERTS, N_DP)
    pair_counts = pair_counts.reshape(EXPERTS, N_DP)
    tile_ends = jnp.cumsum(expert_tiles).astype(jnp.int32)
    tile_expert = jnp.sum((tile_ends[None, :] <= jnp.arange(TILES, dtype=jnp.int32)[:, None]).astype(jnp.int32), 1).astype(jnp.int32)
    block_cap = MOST * N_EXPERT
    padded = jnp.concatenate([sorted_ids, jnp.zeros((block_cap,), jnp.int32)])

    def take_block(start):
        return lax.dynamic_slice(padded, (start.astype(jnp.int32),), (block_cap,))

    def tile_step(totals, tile_index):
        grad_x, grad_g = totals
        expert = tile_expert[tile_index]
        picked = jax.vmap(take_block)(pair_starts[expert]).reshape(-1)
        live_rows = (jnp.arange(block_cap, dtype=jnp.int32)[None, :] < pair_counts[expert][:, None]).reshape(-1)
        token_rows = picked // TOP
        weight = jnp.where(live_rows, gate_flat[picked], jnp.zeros((), gate_flat.dtype)).astype(jnp.float32)
        inputs = jnp.where(live_rows[:, None], tokens[token_rows], jnp.zeros((), tokens.dtype))
        upstream = jnp.where(live_rows[:, None], grad_out[token_rows], jnp.zeros((), grad_out.dtype))
        hidden = jnp.dot(inputs, w_in[tile_index], preferred_element_type=jnp.float32)
        activation, gelu_slope = gelu_pair(hidden)
        back_proj = jnp.dot(upstream, w_out[tile_index].T, preferred_element_type=jnp.float32)
        gate_part = jnp.sum(activation * back_proj, 1).astype(jnp.bfloat16)
        grad_hidden = (weight[:, None] * back_proj * gelu_slope).astype(jnp.bfloat16)
        gated_act = (weight[:, None] * activation).astype(jnp.bfloat16)
        token_part = jnp.dot(grad_hidden, w_in[tile_index].T, preferred_element_type=jnp.float32).astype(jnp.bfloat16)
        in_partial = jnp.einsum("prd,prh->pdh", inputs.reshape(N_DP, block_cap, D).astype(jnp.float32), grad_hidden.reshape(N_DP, block_cap, TILE).astype(jnp.float32))
        out_partial = jnp.einsum("prh,prd->phd", gated_act.reshape(N_DP, block_cap, TILE).astype(jnp.float32), upstream.reshape(N_DP, block_cap, D).astype(jnp.float32))
        grad_in_w = jnp.sum(lax.optimization_barrier(in_partial.astype(jnp.bfloat16)).astype(jnp.float32), 0)
        grad_out_w = jnp.sum(lax.optimization_barrier(out_partial.astype(jnp.bfloat16)).astype(jnp.float32), 0)
        grad_x = grad_x.at[token_rows].add(jnp.where(live_rows[:, None], token_part.astype(jnp.float32), jnp.float32(0.0)))
        grad_g = grad_g.at[picked].add(jnp.where(live_rows, gate_part.astype(jnp.float32), jnp.float32(0.0)))
        return (grad_x, grad_g), (grad_in_w, grad_out_w)

    start_totals = (jnp.zeros((TOKENS, D), jnp.float32), jnp.zeros((TOKENS * TOP,), jnp.float32))
    (grad_x, grad_g), (grad_w_in, grad_w_out) = lax.scan(tile_step, start_totals, jnp.arange(TILES, dtype=jnp.int32))
    return grad_x.astype(jnp.bfloat16), grad_g.reshape(TOKENS, TOP), grad_w_in, grad_w_out
```

```python
import functools

import jax
import jax.numpy as jnp
from jax import lax
from jax.experimental import pallas as pl
from jax.experimental.pallas import tpu as pltpu
from jax.sharding import PartitionSpec as P

MESH = pl.DeviceIdType.MESH
BF16, F32 = jnp.bfloat16, jnp.float32

NY, NX = 8, 4
TOK = 128
D, TILE = 2048, 256
TILES, TILES_DEV = 64, 2
MOST = 13
CHUNK = 512
NCH = D // CHUNK
ROWS = 112
SEL = NX * TILES_DEV * ROWS
ALL_TOK = NY * TOK
HALF = TOK // 2


def my_place():
    e = lax.axis_index("expert")
    return e // NX, e % NX


def at(y, x):
    return {"expert": lax.rem(y + NY, NY) * NX + lax.rem(x + NX, NX)}


def greet():
    y, x = my_place()
    barrier = pltpu.get_barrier_semaphore()
    others = [at(y + 1, x), at(y - 1, x)] + [at(y, x + k) for k in range(1, NX)]
    for other in others:
        pl.semaphore_signal(barrier, inc=1, device_id=other, device_id_type=MESH)
    pl.semaphore_wait(barrier, len(others))


def dot(a, b, dims):
    return lax.dot_general(a, b, (dims, ((), ())), preferred_element_type=F32)


def tile_experts(tiles):
    n = tiles.shape[1]
    upto = lax.broadcasted_iota(jnp.int32, (n, n), 1) <= lax.broadcasted_iota(jnp.int32, (n, n), 0)
    ends = jnp.sum(jnp.where(upto, tiles.astype(F32), 0.0), axis=1, keepdims=True)
    lane = lax.broadcasted_iota(jnp.int32, (n, 128), 1) % TILES
    return jnp.sum(jnp.where(ends <= lane.astype(F32), 1.0, 0.0), axis=0, keepdims=True)


def token_table(routes, gates, tiles):
    of_tile = tile_experts(tiles)
    named = jnp.zeros((TOK, 128), F32)
    gate = jnp.zeros((TOK, 128), F32)
    for k in range(routes.shape[1]):
        hit = routes[:, k : k + 1].astype(F32) == of_tile
        named = jnp.where(hit, 1.0, named)
        gate = jnp.where(hit, gates[:, k : k + 1].astype(F32), gate)
    upto = lax.broadcasted_iota(jnp.int32, (TOK, TOK), 1) <= lax.broadcasted_iota(jnp.int32, (TOK, TOK), 0)
    rank = dot(jnp.where(upto, 1.0, 0.0).astype(BF16), named.astype(BF16), ((1,), (0,)))
    slot = jnp.where(named > 0.0, rank - 1.0, -1.0)
    lane = lax.broadcasted_iota(jnp.int32, (TOK, 128), 1)
    return jnp.where(lane < TILES, slot, gate).astype(BF16)


def fill_selection(table, sel):
    y, x = my_place()
    a = lax.broadcasted_iota(jnp.int32, (8, 128), 0)
    lane = lax.broadcasted_iota(jnp.int32, (8, 128), 1)
    want = (y * NX + lax.rem(x + a // TILES_DEV, NX)) * TILES_DEV + a % TILES_DEV
    pick = jnp.where(lane == want, 1.0, 0.0).astype(BF16)
    slots = dot(pick, table, ((1,), (1,)))
    source = lax.broadcasted_iota(jnp.int32, (8, ALL_TOK), 1) // TOK
    place = jnp.where(slots >= 0.0, slots + (source * MOST).astype(F32), -1.0)
    row = lax.broadcasted_iota(jnp.int32, (ROWS, ALL_TOK), 0).astype(F32)
    for a in range(NX * TILES_DEV):
        sel[a * ROWS : (a + 1) * ROWS, :] = jnp.where(place[a : a + 1, :] == row, 1.0, 0.0).astype(BF16)


def dispatch_kernel(tok, dy, routes, gates, tiles, rx, rm, sel, xg, mg, sx, sm, near, ys, yr, xs, xr):
    y, x = my_place()
    chunks = 1 + 2 * NCH

    def gathered(c):
        return mg if c == 0 else xg.at[c - 1]

    def ring(c, hop, way):
        here = hop - 1 if way == 0 else (NY - (hop - 1)) % NY
        there = hop if way == 0 else NY - hop
        src, dst = gathered(c).at[here], gathered(c).at[there]
        if hop == NY // 2:
            rows = pl.ds(way * HALF, HALF)
            src, dst = src.at[rows], dst.at[rows]
        return pltpu.make_async_remote_copy(
            src_ref=src,
            dst_ref=dst,
            send_sem=ys.at[c, hop - 1, way],
            recv_sem=yr.at[c, hop - 1, way],
            device_id=at(y + 1 - 2 * way, x),
            device_id_type=MESH,
        )

    def across(c, k):
        src = sm.at[k] if c == 0 else sx.at[c - 1, k]
        dst = rm.at[:, k] if c == 0 else rx.at[c - 1, :, k]
        if k == 0:
            return pltpu.make_async_copy(src, dst, xs.at[c, 0])
        return pltpu.make_async_remote_copy(
            src_ref=src,
            dst_ref=dst,
            send_sem=xs.at[c, k],
            recv_sem=xr.at[c, k],
            device_id=at(y, x + k),
            device_id_type=MESH,
        )

    own = []
    for c in range(2 * NCH):
        src = (tok if c < NCH else dy).at[:, pl.ds((c % NCH) * CHUNK, CHUNK)]
        own.append(pltpu.make_async_copy(src, xg.at[c, 0], near.at[c]))
        own[-1].start()
    mg[0] = token_table(routes[...], gates[...], tiles[...])
    greet()

    for s in range(chunks + NY // 2 + 1):
        for c in range(chunks):
            if c == s:
                if c > 0:
                    own[c - 1].wait()
                for way in range(2):
                    ring(c, 1, way).start()
        for c in range(chunks):
            hop = s - c
            if 1 <= hop <= NY // 2:
                for way in range(2):
                    ring(c, hop, way).wait_recv()
                    if hop < NY // 2:
                        ring(c, hop + 1, way).start()
            if hop == NY // 2:
                if c == 0:
                    fill_selection(mg[...].reshape(ALL_TOK, 128), sel)
                for k in (2, 1, 3, 0):
                    part = sel[k * 2 * ROWS : (k + 1) * 2 * ROWS, :]
                    rows = dot(part, gathered(c)[...].reshape(ALL_TOK, -1), ((1,), (0,))).astype(BF16)
                    if c == 0:
                        sm[k] = rows.reshape(TILES_DEV, ROWS, 128)
                    else:
                        sx[c - 1, k] = rows.reshape(TILES_DEV, ROWS, CHUNK)
                    across(c, k).start()
    for c in range(chunks):
        across(c, 0).wait()
        for k in range(1, NX):
            across(c, k).wait()
        for hop in range(1, NY // 2 + 1):
            for way in range(2):
                ring(c, hop, way).wait_send()


def dispatch(tokens, grad_out, routes, gates, tiles):
    chunks = 1 + 2 * NCH
    vmem, anywhere = pl.BlockSpec(memory_space=pltpu.VMEM), pl.BlockSpec(memory_space=pl.ANY)
    return pl.pallas_call(
        dispatch_kernel,
        out_shape=(
            jax.ShapeDtypeStruct((2 * NCH, TILES_DEV, NX, ROWS, CHUNK), BF16),
            jax.ShapeDtypeStruct((TILES_DEV, NX, ROWS, 128), BF16),
            jax.ShapeDtypeStruct((SEL, ALL_TOK), BF16),
        ),
        in_specs=[anywhere, anywhere, vmem, vmem, vmem],
        out_specs=(anywhere, anywhere, vmem),
        scratch_shapes=[
            pltpu.VMEM((2 * NCH, NY, TOK, CHUNK), BF16),
            pltpu.VMEM((NY, TOK, 128), BF16),
            pltpu.VMEM((2 * NCH, NX, TILES_DEV, ROWS, CHUNK), BF16),
            pltpu.VMEM((NX, TILES_DEV, ROWS, 128), BF16),
            pltpu.SemaphoreType.DMA((2 * NCH,)),
            pltpu.SemaphoreType.DMA((chunks, NY // 2, 2)),
            pltpu.SemaphoreType.DMA((chunks, NY // 2, 2)),
            pltpu.SemaphoreType.DMA((chunks, NX)),
            pltpu.SemaphoreType.DMA((chunks, NX)),
        ],
        compiler_params=pltpu.CompilerParams(
            collective_id=0, has_side_effects=True, vmem_limit_bytes=50 << 20
        ),
        name="dispatch",
    )(tokens, grad_out, routes, gates, tiles)


def gelu_pair(v):
    inner = 0.7978845608 * (v + 0.044715 * v * v * v)
    t = jnp.tanh(inner)
    act = 0.5 * v * (1.0 + t)
    slope = 0.5 * (1.0 + t) + 0.5 * v * (1.0 - t * t) * (0.7978845608 * (1.0 + 3.0 * 0.044715 * v * v))
    return act, slope


def compute_kernel(rx, rm, w_in, w_out, tp, gp, in_part, out_part):
    e = lax.axis_index("expert")
    rows = NX * ROWS
    lane = lax.broadcasted_iota(jnp.int32, (rows, 128), 1)
    for j in range(TILES_DEV):
        hidden = jnp.zeros((rows, TILE), F32)
        back = jnp.zeros((rows, TILE), F32)
        for c in range(NCH):
            cols = slice(c * CHUNK, (c + 1) * CHUNK)
            hidden += dot(rx[c, j].reshape(rows, CHUNK), w_in[j, cols, :], ((1,), (0,)))
            back += dot(rx[NCH + c, j].reshape(rows, CHUNK), w_out[j, :, cols], ((1,), (1,)))
        tile = e * TILES_DEV + j
        table = rm[j].reshape(rows, 128).astype(F32)
        gate = jnp.sum(jnp.where(lane == TILES + tile, table, 0.0), axis=1, keepdims=True)
        act, slope = gelu_pair(hidden)
        gate_part = jnp.sum(act * back, axis=1, keepdims=True)
        gp[j] = jnp.where(lane == tile, gate_part, 0.0).astype(BF16).reshape(NX, ROWS, 128)
        grad_hidden = (gate * back * slope).astype(BF16)
        gated_act = (gate * act).astype(BF16)
        for c in range(NCH):
            cols = slice(c * CHUNK, (c + 1) * CHUNK)
            tp[c, j] = dot(grad_hidden, w_in[j, cols, :], ((1,), (1,))).astype(BF16).reshape(NX, ROWS, CHUNK)
            in_part[j, cols, :] = dot(rx[c, j].reshape(rows, CHUNK), grad_hidden, ((0,), (0,))).astype(BF16)
            out_part[j, :, cols] = dot(gated_act, rx[NCH + c, j].reshape(rows, CHUNK), ((0,), (0,))).astype(BF16)


def compute(rx, rm, w_in, w_out):
    vmem = pl.BlockSpec(memory_space=pltpu.VMEM)
    return pl.pallas_call(
        compute_kernel,
        out_shape=(
            jax.ShapeDtypeStruct((NCH, TILES_DEV, NX, ROWS, CHUNK), BF16),
            jax.ShapeDtypeStruct((TILES_DEV, NX, ROWS, 128), BF16),
            jax.ShapeDtypeStruct((TILES_DEV, D, TILE), BF16),
            jax.ShapeDtypeStruct((TILES_DEV, TILE, D), BF16),
        ),
        in_specs=[vmem] * 4,
        out_specs=(vmem,) * 4,
        compiler_params=pltpu.CompilerParams(vmem_limit_bytes=50 << 20),
        name="compute",
    )(rx, rm, w_in, w_out)


def combine_kernel(tp, gp, sel, routes, tiles, gt, gg, bx, bm, pt, pm, ob, om, ib, im, xs, xr, ys, yr):
    y, x = my_place()
    chunks = 1 + NCH

    def across(c, k):
        src = gp.at[:, k] if c == 0 else tp.at[c - 1, :, k]
        dst = bm.at[k] if c == 0 else bx.at[c - 1, k]
        if k == 0:
            return pltpu.make_async_copy(src, dst, xs.at[c, 0])
        return pltpu.make_async_remote_copy(
            src_ref=src,
            dst_ref=dst,
            send_sem=xs.at[c, k],
            recv_sem=xr.at[c, k],
            device_id=at(y, x - k),
            device_id_type=MESH,
        )

    def stage(c, out):
        if c == 0:
            return om if out else im
        return (ob if out else ib).at[c - 1]

    def ring(c, hop, way):
        src, dst = stage(c, True).at[hop - 1, way], stage(c, False).at[hop - 1, way]
        if hop == 1:
            rows = pl.ds(way * HALF, HALF)
            src, dst = src.at[rows], dst.at[rows]
        return pltpu.make_async_remote_copy(
            src_ref=src,
            dst_ref=dst,
            send_sem=ys.at[c, hop - 1, way],
            recv_sem=yr.at[c, hop - 1, way],
            device_id=at(y - 1 + 2 * way, x),
            device_id_type=MESH,
        )

    def partial(c):
        return pm if c == 0 else pt.at[c - 1]

    greet()
    for c in range(chunks):
        for k in (2, 1, 3, 0):
            across(c, k).start()

    for s in range(chunks + NY // 2):
        for c in range(chunks):
            hop = s - c
            if hop == 0:
                across(c, 0).wait()
                for k in range(1, NX):
                    across(c, k).wait_recv()
                back = (bm if c == 0 else bx.at[c - 1])[...].reshape(SEL, -1)
                partial(c)[...] = dot(sel[...], back, ((0,), (0,))).reshape(NY, TOK, -1)
                for way in range(2):
                    rows = slice(way * HALF, (way + 1) * HALF)
                    stage(c, True)[0, way, rows] = partial(c)[NY // 2, rows].astype(BF16)
                    ring(c, 1, way).start()
            if 1 <= hop < NY // 2:
                for way in range(2):
                    ring(c, hop, way).wait_recv()
                    slot = NY // 2 - hop if way == 0 else NY // 2 + hop
                    if hop == 1:
                        rows = slice(way * HALF, (way + 1) * HALF)
                        rest = slice((1 - way) * HALF, (2 - way) * HALF)
                        stage(c, True)[hop, way, rows] = (
                            partial(c)[slot, rows] + stage(c, False)[0, way, rows].astype(F32)
                        ).astype(BF16)
                        stage(c, True)[hop, way, rest] = partial(c)[slot, rest].astype(BF16)
                    else:
                        stage(c, True)[hop, way] = (
                            partial(c)[slot] + stage(c, False)[hop - 1, way].astype(F32)
                        ).astype(BF16)
                    ring(c, hop + 1, way).start()
            if hop == NY // 2:
                total = partial(c)[0]
                for way in range(2):
                    ring(c, hop, way).wait_recv()
                    total += stage(c, False)[hop - 1, way].astype(F32)
                if c == 0:
                    lane = lax.broadcasted_iota(jnp.int32, (TOK, 128), 1)
                    of_tile = jnp.where(lane < TILES, tile_experts(tiles[...]), -1.0)
                    for k in range(routes.shape[1]):
                        mine = routes[:, k : k + 1].astype(F32) == of_tile
                        gg[:, k : k + 1] = jnp.sum(jnp.where(mine, total, 0.0), axis=1, keepdims=True)
                else:
                    gt[:, (c - 1) * CHUNK : c * CHUNK] = total.astype(BF16)
    for c in range(chunks):
        for k in range(1, NX):
            across(c, k).wait_send()
        for hop in range(1, NY // 2 + 1):
            for way in range(2):
                ring(c, hop, way).wait_send()


def combine(tp, gp, sel, routes, tiles):
    chunks = 1 + NCH
    vmem, anywhere = pl.BlockSpec(memory_space=pltpu.VMEM), pl.BlockSpec(memory_space=pl.ANY)
    hops = NY // 2
    return pl.pallas_call(
        combine_kernel,
        out_shape=(
            jax.ShapeDtypeStruct((TOK, D), BF16),
            jax.ShapeDtypeStruct(routes.shape, F32),
        ),
        in_specs=[anywhere, anywhere, vmem, vmem, vmem],
        out_specs=(vmem, vmem),
        scratch_shapes=[
            pltpu.VMEM((NCH, NX, TILES_DEV, ROWS, CHUNK), BF16),
            pltpu.VMEM((NX, TILES_DEV, ROWS, 128), BF16),
            pltpu.VMEM((NCH, NY, TOK, CHUNK), F32),
            pltpu.VMEM((NY, TOK, 128), F32),
            pltpu.VMEM((NCH, hops, 2, TOK, CHUNK), BF16),
            pltpu.VMEM((hops, 2, TOK, 128), BF16),
            pltpu.VMEM((NCH, hops, 2, TOK, CHUNK), BF16),
            pltpu.VMEM((hops, 2, TOK, 128), BF16),
            pltpu.SemaphoreType.DMA((chunks, NX)),
            pltpu.SemaphoreType.DMA((chunks, NX)),
            pltpu.SemaphoreType.DMA((chunks, hops, 2)),
            pltpu.SemaphoreType.DMA((chunks, hops, 2)),
        ],
        compiler_params=pltpu.CompilerParams(
            collective_id=1, has_side_effects=True, vmem_limit_bytes=50 << 20
        ),
        name="combine",
    )(tp, gp, sel, routes, tiles)


def on_device(tokens, grad_out, routes, gates, expert_tiles, w_in, w_out):
    tiles = expert_tiles.reshape(1, -1)
    full_in = lax.all_gather(w_in, "dp", axis=1, tiled=True)
    full_out = lax.all_gather(w_out, "dp", axis=2, tiled=True)
    rx, rm, sel = dispatch(tokens, grad_out, routes, gates, tiles)
    tp, gp, in_part, out_part = compute(rx, rm, full_in, full_out)
    grad_in = lax.psum_scatter(in_part, "dp", scatter_dimension=1, tiled=True)
    grad_out_w = lax.psum_scatter(out_part, "dp", scatter_dimension=2, tiled=True)
    grad_tokens, grad_gates = combine(tp, gp, sel, routes, tiles)
    return grad_tokens, grad_gates, grad_in.astype(F32), grad_out_w.astype(F32)


def solution(mesh):
    rows = P(("dp", "expert"), None)
    w_in, w_out = P("expert", "dp", None), P("expert", None, "dp")
    return jax.shard_map(
        on_device,
        mesh=mesh,
        in_specs=(rows, rows, rows, rows, P(), w_in, w_out),
        out_specs=(rows, rows, w_in, w_out),
        check_vma=False,
    )
```

```python
import jax
import jax.numpy as jnp
from jax import lax
from jax.experimental import pallas as pl
from jax.experimental.pallas import tpu as pltpu
from jax.sharding import PartitionSpec as P

MESH = pl.DeviceIdType.MESH
BF16, F32 = jnp.bfloat16, jnp.float32

NY, NX = 8, 4
TOK = 128
D, TILE = 2048, 256
TILES, TILES_DEV = 64, 2
MOST = 13
CHUNK = 512
NCH = D // CHUNK
ROWS = 112
SEL = NX * TILES_DEV * ROWS
ALL_TOK = NY * TOK
NZ = 8
SLICE = D // (2 * NZ)
HALF = TOK // 2


def my_place():
    e, p = lax.axis_index("expert"), lax.axis_index("dp")
    return e // NX, e % NX, p // 2, p % 2


def at(y, x):
    return {"expert": lax.rem(y + NY, NY) * NX + lax.rem(x + NX, NX)}


def at_z(z, core):
    return {"dp": lax.rem(z + NZ, NZ) * 2 + core}


def greet():
    y, x, z, core = my_place()
    barrier = pltpu.get_barrier_semaphore()
    others = [at(y + 1, x), at(y - 1, x)] + [at(y, x + k) for k in range(1, NX)]
    others += [at_z(z + 1, core), at_z(z - 1, core), at_z(z, 1 - core)]
    for other in others:
        pl.semaphore_signal(barrier, inc=1, device_id=other, device_id_type=MESH)
    pl.semaphore_wait(barrier, len(others))


def dot(a, b, dims):
    return lax.dot_general(a, b, (dims, ((), ())), preferred_element_type=F32)


def send(src, dst, send_sem, recv_sem, to):
    return pltpu.make_async_remote_copy(
        src_ref=src, dst_ref=dst, send_sem=send_sem, recv_sem=recv_sem, device_id=to, device_id_type=MESH
    )


def iota(shape, dim):
    return lax.broadcasted_iota(jnp.int32, shape, dim)


def columns(rows):
    eye = jnp.where(iota((TOK, TOK), 0) == iota((TOK, TOK), 1), 1.0, 0.0).astype(BF16)
    return dot(eye, rows.astype(F32).astype(BF16), ((1,), (1,)))


def tile_experts(tiles):
    n = tiles.shape[1]
    upto = iota((n, n), 1) <= iota((n, n), 0)
    ends = jnp.sum(jnp.where(upto, tiles.astype(F32), 0.0), axis=1, keepdims=True)
    lane = iota((n, 128), 1) % TILES
    return jnp.sum(jnp.where(ends <= lane.astype(F32), 1.0, 0.0), axis=0, keepdims=True)


def token_table(routes, gates, tiles):
    of_tile = tile_experts(tiles)
    named = jnp.zeros((TOK, 128), F32)
    gate = jnp.zeros((TOK, 128), F32)
    for k in range(routes.shape[1]):
        hit = routes[:, k : k + 1] == of_tile
        named = jnp.where(hit, 1.0, named)
        gate = jnp.where(hit, gates[:, k : k + 1], gate)
    upto = iota((TOK, TOK), 1) <= iota((TOK, TOK), 0)
    rank = dot(jnp.where(upto, 1.0, 0.0).astype(BF16), named.astype(BF16), ((1,), (0,)))
    slot = jnp.where(named > 0.0, rank - 1.0, -1.0)
    return jnp.where(iota((TOK, 128), 1) < TILES, slot, gate).astype(BF16)


def fill_selection(table, sel):
    y, x, _, _ = my_place()
    a = iota((8, 128), 0)
    want = (y * NX + lax.rem(x + a // TILES_DEV, NX)) * TILES_DEV + a % TILES_DEV
    pick = jnp.where(iota((8, 128), 1) == want, 1.0, 0.0).astype(BF16)
    slots = dot(pick, table, ((1,), (1,)))
    source = iota((8, ALL_TOK), 1) // TOK
    place = jnp.where(slots >= 0.0, slots + (source * MOST).astype(F32), -1.0)
    row = iota((ROWS, ALL_TOK), 0).astype(F32)
    for a in range(NX * TILES_DEV):
        sel[a * ROWS : (a + 1) * ROWS, :] = jnp.where(place[a : a + 1, :] == row, 1.0, 0.0).astype(BF16)


def gelu_pair(v):
    t = jnp.tanh(0.7978845608 * (v + 0.044715 * v * v * v))
    act = 0.5 * v * (1.0 + t)
    slope = 0.5 * (1.0 + t) + 0.5 * v * (1.0 - t * t) * (0.7978845608 * (1.0 + 3.0 * 0.044715 * v * v))
    return act, slope


OUT = 1 + 2 * NCH
BACK = 1 + NCH
HY, HZ = NY // 2, NZ // 2
ALL_ROWS = NX * ROWS


def layer_kernel(
    tok, dy, routes, gates, tiles, w_in, w_out,
    gt, gg, gin, gout,
    xg, mg, sx, sm, rx, rm, sel, win, wout, hidden, back, gh, ga,
    gp, bx, bm, pm, om, ib, im, parts_in, parts_out, twin_in, twin_out, zo_in, zi_in, zo_out, zi_out,
    near, ys, yr, xs, xr, ws, wr, cs, cr, qs, qr, rs, rr, ks, kr, zs, zr,
):
    y, x, z, core = my_place()
    e = lax.axis_index("expert")

    def gathered(c):
        return mg if c == 0 else xg.at[c - 1]

    def ring(c, hop, way):
        here = hop - 1 if way == 0 else (NY - (hop - 1)) % NY
        there = hop if way == 0 else NY - hop
        src, dst = gathered(c).at[here], gathered(c).at[there]
        if hop == HY:
            rows = pl.ds(way * HALF, HALF)
            src, dst = src.at[rows], dst.at[rows]
        return send(src, dst, ys.at[c, hop - 1, way], yr.at[c, hop - 1, way], at(y + 1 - 2 * way, x))

    def across(c, k):
        src = sm.at[k] if c == 0 else sx.at[c - 1, k]
        dst = rm.at[:, k] if c == 0 else rx.at[c - 1, :, k]
        return send(src, dst, xs.at[c, k], xr.at[c, k], at(y, x + k))

    def piece(a, home, tile):
        p = pl.multiple_of((lax.rem(home + 2 * NZ, NZ) * 2 + core) * SLICE, SLICE)
        j = slice(None) if tile is None else pl.ds(tile, 1)
        return win.at[j, pl.ds(p, SLICE), :] if a == 0 else wout.at[j, :, pl.ds(p, SLICE)]

    def weights(a, hop, way):
        part = piece(a, z - (hop - 1) * (1 - 2 * way), way if hop == HZ else None)
        return send(part, part, ws.at[a, hop - 1, way], wr.at[a, hop - 1, way], at_z(z + 1 - 2 * way, core))

    def twin(a, hop, way):
        part = piece(a, z - hop * (1 - 2 * way), way if hop == HZ else None)
        return send(part, part, cs.at[a, hop, way], cr.at[a, hop, way], at_z(z, 1 - core))

    own = []
    for c in range(2 * NCH):
        src = (tok if c < NCH else dy).at[:, pl.ds((c % NCH) * CHUNK, CHUNK)]
        own.append(pltpu.make_async_copy(src, xg.at[c, 0], near.at[c]))
    for a, src in ((0, w_in), (1, w_out)):
        own.append(pltpu.make_async_copy(src, piece(a, z, None), near.at[2 * NCH + a]))
    for copy in own:
        copy.start()
    route_cols = columns(routes[...])
    mg[0] = token_table(route_cols, columns(gates[...]), tiles[...])
    greet()

    hidden[...] = jnp.zeros_like(hidden)
    back[...] = jnp.zeros_like(back)
    for s in range(OUT + HY + 2):
        if s < OUT:
            if s > 0:
                own[s - 1].wait()
            for way in range(2):
                ring(s, 1, way).start()
        for c in range(OUT):
            hop = s - c
            if 1 <= hop <= HY:
                for way in range(2):
                    ring(c, hop, way).wait_recv()
                    if hop < HY:
                        ring(c, hop + 1, way).start()
        if s <= HZ:
            for a in range(2):
                if s == 0:
                    own[2 * NCH + a].wait()
                for way in range(2):
                    if s > 0:
                        weights(a, s, way).wait_recv()
                    if s > 0 or way == 0:
                        twin(a, s, way).start()
                    if s < HZ:
                        weights(a, s + 1, way).start()
        if s == HZ + 2:
            for a in range(2):
                for hop in range(HZ + 1):
                    for way in range(2 if hop > 0 else 1):
                        twin(a, hop, way).wait_recv()
        c = s - HY
        if 0 <= c < OUT:
            if c == 0:
                fill_selection(mg[...].reshape(ALL_TOK, 128), sel)
            for k in (2, 1, 3, 0):
                part = sel[k * 2 * ROWS : (k + 1) * 2 * ROWS, :]
                rows = dot(part, gathered(c)[...].reshape(ALL_TOK, -1), ((1,), (0,))).astype(BF16)
                rows = rows.reshape(TILES_DEV, ROWS, -1)
                if k == 0 and c == 0:
                    rm[:, 0] = rows
                elif k == 0:
                    rx[c - 1, :, 0] = rows
                elif c == 0:
                    sm[k] = rows
                else:
                    sx[c - 1, k] = rows
                if k > 0:
                    across(c, k).start()
        c = s - HY - 2
        if 0 <= c < OUT:
            for k in range(1, NX):
                across(c, k).wait_recv()
            for j in range(TILES_DEV):
                if c > 0:
                    cols = slice((c - 1) % NCH * CHUNK, ((c - 1) % NCH + 1) * CHUNK)
                    rows = rx[c - 1, j].reshape(ALL_ROWS, CHUNK)
                    if c <= NCH:
                        hidden[j] += dot(rows, win[j, cols, :], ((1,), (0,)))
                    else:
                        back[j] += dot(rows, wout[j, :, cols], ((1,), (1,)))

    def return_x(c, k):
        src = gp.at[k] if c == 0 else sx.at[c - 1, k]
        dst = bm.at[k] if c == 0 else bx.at[c - 1, k]
        return send(src, dst, qs.at[c, k], qr.at[c, k], at(y, x - k))

    def partial(c):
        return pm if c == 0 else xg.at[c - 1]

    def outgoing(c, hop, way):
        return om.at[hop - 1, way] if c == 0 else xg.at[NCH + c - 1, (hop - 1) * 2 + way]

    def incoming(c, hop, way):
        return im.at[hop - 1, way] if c == 0 else ib.at[c - 1, hop - 1, way]

    def return_y(c, hop, way):
        src, dst = outgoing(c, hop, way), incoming(c, hop, way)
        if hop == 1:
            rows = pl.ds(way * HALF, HALF)
            src, dst = src.at[rows], dst.at[rows]
        return send(src, dst, rs.at[c, hop - 1, way], rr.at[c, hop - 1, way], at(y - 1 + 2 * way, x))

    def swap(a):
        src, dst = (parts_in, twin_in) if a == 0 else (parts_out, twin_out)
        return send(src.at[:, 1 - core], dst, ks.at[a], kr.at[a], at_z(z, 1 - core))

    def return_z(a, hop, way):
        src, dst = (zo_in, zi_in) if a == 0 else (zo_out, zi_out)
        src, dst = src.at[hop - 1, way], dst.at[hop - 1, way]
        if hop == 1:
            src, dst = src.at[pl.ds(way, 1)], dst.at[pl.ds(way, 1)]
        return send(src, dst, zs.at[a, hop - 1, way], zr.at[a, hop - 1, way], at_z(z - 1 + 2 * way, core))

    def chip_sum(a, slot, tile):
        home = lax.rem(z - slot + NZ, NZ)
        mine, other = (parts_in, twin_in) if a == 0 else (parts_out, twin_out)
        return mine[home, core, tile].astype(F32) + other[home, tile].astype(F32)

    lane = iota((ALL_ROWS, 128), 1)
    for j in range(TILES_DEV):
        tile = e * TILES_DEV + j
        table = rm[j].reshape(ALL_ROWS, 128).astype(F32)
        gate = jnp.sum(jnp.where(lane == TILES + tile, table, 0.0), axis=1, keepdims=True)
        act, slope = gelu_pair(hidden[j])
        gate_part = jnp.sum(act * back[j], axis=1, keepdims=True)
        terms = jnp.where(lane == tile, gate_part, 0.0).astype(BF16).reshape(NX, ROWS, 128)
        bm[0, j] = terms[0]
        for k in range(1, NX):
            gp[k, j] = terms[k]
        gh[j] = (gate * back[j] * slope).astype(BF16)
        ga[j] = (gate * act).astype(BF16)
    for c in range(BACK):
        if c > 0:
            cols = slice((c - 1) * CHUNK, c * CHUNK)
            for k in range(1, NX):
                across(c, k).wait_send()
            for j in range(TILES_DEV):
                rows = dot(gh[j], win[j, cols, :], ((1,), (1,))).astype(BF16).reshape(NX, ROWS, CHUNK)
                bx[c - 1, 0, j] = rows[0]
                for k in range(1, NX):
                    sx[c - 1, k, j] = rows[k]
        for k in (2, 1, 3):
            return_x(c, k).start()
    for c in range(NCH):
        for j in range(TILES_DEV):
            rows = rx[c, j].reshape(ALL_ROWS, CHUNK)
            part = dot(rows, gh[j], ((0,), (0,))).astype(BF16)
            for i in range(CHUNK // SLICE):
                q = c * (CHUNK // SLICE) + i
                parts_in[q // 2, q % 2, j] = part[i * SLICE : (i + 1) * SLICE, :]
    swap(0).start()
    for c in range(NCH):
        for j in range(TILES_DEV):
            rows = rx[NCH + c, j].reshape(ALL_ROWS, CHUNK)
            part = dot(ga[j], rows, ((0,), (0,))).astype(BF16)
            for i in range(CHUNK // SLICE):
                q = c * (CHUNK // SLICE) + i
                parts_out[q // 2, q % 2, j] = part[:, i * SLICE : (i + 1) * SLICE]
    swap(1).start()
    for c in range(OUT):
        for hop in range(1, HY + 1):
            for way in range(2):
                ring(c, hop, way).wait_send()

    for s in range(BACK + HY):
        for c in range(BACK):
            hop = s - c
            if 1 <= hop < HY:
                for way in range(2):
                    return_y(c, hop, way).wait_recv()
                    slot = HY - hop if way == 0 else HY + hop
                    if hop == 1:
                        rows = slice(way * HALF, (way + 1) * HALF)
                        rest = slice((1 - way) * HALF, (2 - way) * HALF)
                        outgoing(c, 2, way)[rows] = (
                            partial(c)[slot, rows].astype(F32) + incoming(c, 1, way)[rows].astype(F32)
                        ).astype(BF16)
                        outgoing(c, 2, way)[rest] = partial(c)[slot, rest]
                    else:
                        outgoing(c, hop + 1, way)[...] = (
                            partial(c)[slot].astype(F32) + incoming(c, hop, way)[...].astype(F32)
                        ).astype(BF16)
                    return_y(c, hop + 1, way).start()
            if hop == HY:
                total = partial(c)[0].astype(F32)
                for way in range(2):
                    return_y(c, hop, way).wait_recv()
                    total += incoming(c, hop, way)[...].astype(F32)
                if c == 0:
                    of_tile = jnp.where(iota((TOK, 128), 1) < TILES, tile_experts(tiles[...]), -1.0)
                    cols = columns(routes[...])
                    ones = jnp.ones((8, 128), BF16)
                    for k in range(routes.shape[0]):
                        mine = jnp.where(cols[:, k : k + 1] == of_tile, total, 0.0).astype(BF16)
                        gg[k : k + 1, :] = dot(ones, mine, ((1,), (1,)))[0:1, :]
                else:
                    gt[:, (c - 1) * CHUNK : c * CHUNK] = total.astype(BF16)
        for a in range(2):
            if s == 1:
                swap(a).wait_recv()
                for way in range(2):
                    (zo_in if a == 0 else zo_out)[0, way, way] = chip_sum(a, HZ, way).astype(BF16)
                    return_z(a, 1, way).start()
            hop = s - 1
            if 1 <= hop < HZ:
                stage, landed = (zo_in, zi_in) if a == 0 else (zo_out, zi_out)
                for way in range(2):
                    return_z(a, hop, way).wait_recv()
                    slot = HZ - hop if way == 0 else HZ + hop
                    for tile in range(TILES_DEV):
                        value = chip_sum(a, slot, tile)
                        if hop > 1 or tile == way:
                            value += landed[hop - 1, way, tile].astype(F32)
                        stage[hop, way, tile] = value.astype(BF16)
                    return_z(a, hop + 1, way).start()
            if hop == HZ:
                landed = zi_in if a == 0 else zi_out
                for way in range(2):
                    return_z(a, HZ, way).wait_recv()
                for tile in range(TILES_DEV):
                    value = chip_sum(a, 0, tile)
                    for way in range(2):
                        value += landed[HZ - 1, way, tile].astype(F32)
                    (gin if a == 0 else gout)[tile] = value
        if s < BACK:
            c = s
            for k in range(1, NX):
                return_x(c, k).wait_recv()
            rows = (bm if c == 0 else bx.at[c - 1])[...].reshape(SEL, -1)
            partial(c)[...] = dot(sel[...], rows, ((0,), (0,))).astype(BF16).reshape(NY, TOK, -1)
            for way in range(2):
                rows = slice(way * HALF, (way + 1) * HALF)
                outgoing(c, 1, way)[rows] = partial(c)[HY, rows]
                return_y(c, 1, way).start()

    for c in range(OUT):
        if c == 0 or c > NCH:
            for k in range(1, NX):
                across(c, k).wait_send()
    for c in range(BACK):
        for k in range(1, NX):
            return_x(c, k).wait_send()
        for hop in range(1, HY + 1):
            for way in range(2):
                return_y(c, hop, way).wait_send()
    for a in range(2):
        swap(a).wait_send()
        for hop in range(HZ + 1):
            for way in range(2):
                if hop > 0 or way == 0:
                    twin(a, hop, way).wait_send()
                if hop > 0:
                    weights(a, hop, way).wait_send()
                    return_z(a, hop, way).wait_send()


def layer(tokens, grad_out, routes, gates, tiles, w_in, w_out):
    vmem, anywhere = pl.BlockSpec(memory_space=pltpu.VMEM), pl.BlockSpec(memory_space=pl.ANY)
    dma = pltpu.SemaphoreType.DMA

    def hold(*shape):
        return pltpu.VMEM(shape, BF16)

    return pl.pallas_call(
        layer_kernel,
        out_shape=(
            jax.ShapeDtypeStruct((TOK, D), BF16),
            jax.ShapeDtypeStruct(routes.shape, F32),
            jax.ShapeDtypeStruct(w_in.shape, F32),
            jax.ShapeDtypeStruct(w_out.shape, F32),
        ),
        in_specs=[anywhere, anywhere, vmem, vmem, vmem, anywhere, anywhere],
        out_specs=(vmem,) * 4,
        scratch_shapes=[
            hold(2 * NCH, NY, TOK, CHUNK),
            hold(NY, TOK, 128),
            hold(2 * NCH, NX, TILES_DEV, ROWS, CHUNK),
            hold(NX, TILES_DEV, ROWS, 128),
            hold(2 * NCH, TILES_DEV, NX, ROWS, CHUNK),
            hold(TILES_DEV, NX, ROWS, 128),
            hold(SEL, ALL_TOK),
            hold(TILES_DEV, D, TILE),
            hold(TILES_DEV, TILE, D),
            pltpu.VMEM((TILES_DEV, ALL_ROWS, TILE), F32),
            pltpu.VMEM((TILES_DEV, ALL_ROWS, TILE), F32),
            hold(TILES_DEV, ALL_ROWS, TILE),
            hold(TILES_DEV, ALL_ROWS, TILE),
            hold(NX, TILES_DEV, ROWS, 128),
            hold(NCH, NX, TILES_DEV, ROWS, CHUNK),
            hold(NX, TILES_DEV, ROWS, 128),
            hold(NY, TOK, 128),
            hold(HY, 2, TOK, 128),
            hold(NCH, HY, 2, TOK, CHUNK),
            hold(HY, 2, TOK, 128),
            hold(NZ, 2, TILES_DEV, SLICE, TILE),
            hold(NZ, 2, TILES_DEV, TILE, SLICE),
            hold(NZ, TILES_DEV, SLICE, TILE),
            hold(NZ, TILES_DEV, TILE, SLICE),
            hold(HZ, 2, TILES_DEV, SLICE, TILE),
            hold(HZ, 2, TILES_DEV, SLICE, TILE),
            hold(HZ, 2, TILES_DEV, TILE, SLICE),
            hold(HZ, 2, TILES_DEV, TILE, SLICE),
            dma((2 * NCH + 2,)),
            dma((OUT, HY, 2)),
            dma((OUT, HY, 2)),
            dma((OUT, NX)),
            dma((OUT, NX)),
            dma((2, HZ, 2)),
            dma((2, HZ, 2)),
            dma((2, HZ + 1, 2)),
            dma((2, HZ + 1, 2)),
            dma((BACK, NX)),
            dma((BACK, NX)),
            dma((BACK, HY, 2)),
            dma((BACK, HY, 2)),
            dma((2,)),
            dma((2,)),
            dma((2, HZ, 2)),
            dma((2, HZ, 2)),
        ],
        compiler_params=pltpu.CompilerParams(
            collective_id=0, has_side_effects=True, vmem_limit_bytes=60 << 20
        ),
        name="layer",
    )(tokens, grad_out, routes, gates, tiles, w_in, w_out)


def on_device(tokens, grad_out, routes, gates, expert_tiles, w_in, w_out):
    grad_tokens, gates_rows, grad_in, grad_out_w = layer(
        tokens, grad_out, routes.T, gates.T, expert_tiles.reshape(1, -1), w_in, w_out
    )
    return grad_tokens, gates_rows.T, grad_in, grad_out_w


def solution(mesh):
    rows = P(("dp", "expert"), None)
    w_in, w_out = P("expert", "dp", None), P("expert", None, "dp")
    return jax.shard_map(
        on_device,
        mesh=mesh,
        in_specs=(rows, rows, rows, rows, P(), w_in, w_out),
        out_specs=(rows, rows, w_in, w_out),
        check_vma=False,
    )
```

```python
import jax
import jax.numpy as jnp
from jax import lax
from jax.experimental import pallas as pl
from jax.experimental.pallas import tpu as pltpu
from jax.sharding import PartitionSpec as P

MESH = pl.DeviceIdType.MESH
BF16, F32 = jnp.bfloat16, jnp.float32

NY, NX = 8, 4
TOK = 128
D, TILE = 2048, 256
TILES, TILES_DEV = 64, 2
MOST = 13
CHUNK = 512
NCH = D // CHUNK
ROWS = 112
SEL = NX * TILES_DEV * ROWS
ALL_TOK = NY * TOK
NZ = 8
SLICE = D // (2 * NZ)
HALF = TOK // 2


def my_place():
    e, p = lax.axis_index("expert"), lax.axis_index("dp")
    return e // NX, e % NX, p // 2, p % 2


def at(y, x):
    return {"expert": lax.rem(y + NY, NY) * NX + lax.rem(x + NX, NX)}


def at_z(z, core):
    return {"dp": lax.rem(z + NZ, NZ) * 2 + core}


def partners():
    y, x, z, core = my_place()
    others = [at(y + 1, x), at(y - 1, x)] + [at(y, x + k) for k in range(1, NX)]
    others += [at_z(z + 1, core), at_z(z - 1, core), at_z(z, 1 - core)]
    return others


def dot(a, b, dims):
    return lax.dot_general(a, b, (dims, ((), ())), preferred_element_type=F32)


def send(src, dst, send_sem, recv_sem, to):
    return pltpu.make_async_remote_copy(
        src_ref=src, dst_ref=dst, send_sem=send_sem, recv_sem=recv_sem, device_id=to, device_id_type=MESH
    )


def iota(shape, dim):
    return lax.broadcasted_iota(jnp.int32, shape, dim)


def columns(rows):
    eye = jnp.where(iota((TOK, TOK), 0) == iota((TOK, TOK), 1), 1.0, 0.0).astype(BF16)
    return dot(eye, rows.astype(F32).astype(BF16), ((1,), (1,)))


def tile_experts(tiles):
    n = tiles.shape[1]
    upto = iota((n, n), 1) <= iota((n, n), 0)
    ends = jnp.sum(jnp.where(upto, tiles.astype(F32), 0.0), axis=1, keepdims=True)
    lane = iota((n, 128), 1) % TILES
    return jnp.sum(jnp.where(ends <= lane.astype(F32), 1.0, 0.0), axis=0, keepdims=True)


def token_table(routes, gates, tiles):
    of_tile = tile_experts(tiles)
    named = jnp.zeros((TOK, 128), F32)
    gate = jnp.zeros((TOK, 128), F32)
    for k in range(routes.shape[1]):
        hit = routes[:, k : k + 1] == of_tile
        named = jnp.where(hit, 1.0, named)
        gate = jnp.where(hit, gates[:, k : k + 1], gate)
    upto = iota((TOK, TOK), 1) <= iota((TOK, TOK), 0)
    rank = dot(jnp.where(upto, 1.0, 0.0).astype(BF16), named.astype(BF16), ((1,), (0,)))
    slot = jnp.where(named > 0.0, rank - 1.0, -1.0)
    return jnp.where(iota((TOK, 128), 1) < TILES, slot, gate).astype(BF16)


def fill_selection(table, sel):
    y, x, _, _ = my_place()
    a = iota((8, 128), 0)
    want = (y * NX + lax.rem(x + a // TILES_DEV, NX)) * TILES_DEV + a % TILES_DEV
    pick = jnp.where(iota((8, 128), 1) == want, 1.0, 0.0).astype(BF16)
    slots = dot(pick, table, ((1,), (1,)))
    source = iota((8, ALL_TOK), 1) // TOK
    place = jnp.where(slots >= 0.0, slots + (source * MOST).astype(F32), -1.0)
    row = iota((ROWS, ALL_TOK), 0).astype(F32)
    for a in range(NX * TILES_DEV):
        sel[a * ROWS : (a + 1) * ROWS, :] = jnp.where(place[a : a + 1, :] == row, 1.0, 0.0).astype(BF16)


def gelu_pair(v):
    t = jnp.tanh(0.7978845608 * (v + 0.044715 * v * v * v))
    act = 0.5 * v * (1.0 + t)
    slope = 0.5 * (1.0 + t) + 0.5 * v * (1.0 - t * t) * (0.7978845608 * (1.0 + 3.0 * 0.044715 * v * v))
    return act, slope


OUT = [(None, 0, 128), (0, 0, 256), (0, 256, 512)] + [(c, 0, CHUNK) for c in range(1, 2 * NCH - 1)]
OUT += [(2 * NCH - 1, 0, 256), (2 * NCH - 1, 256, 512)]
STARTS = [0, 0, 1, 3, 5, 7, 9, 11, 13, 15, 16]
LAG = 6
BACK = [(None, 0, 128)] + [(c, 0, CHUNK) for c in range(NCH)]
RETURNS = list(range(len(BACK)))
AHEAD = 2
HY, HZ = NY // 2, NZ // 2
ALL_ROWS = NX * ROWS


def layer_kernel(
    tok, dy, routes, gates, tiles, w_in, w_out,
    gt, gg, gin, gout,
    xg, mg, sx, sm, rx, rm, sel, win, wout, hidden, back, gh, ga,
    gp, bx, bm, pm, om, ib, im, parts_in, parts_out, twin_in, twin_out, zo_in, zi_in, zo_out, zi_out,
    near, ys, yr, xs, xr, ws, wr, cs, cr, qs, qr, rs, rr, ks, kr, zs, zr,
):
    y, x, z, core = my_place()
    e = lax.axis_index("expert")

    def gathered(i):
        c, lo, hi = OUT[i]
        return mg if c is None else xg.at[c, :, :, lo:hi]

    def ring(c, hop, way):
        here = hop - 1 if way == 0 else (NY - (hop - 1)) % NY
        there = hop if way == 0 else NY - hop
        src, dst = gathered(c).at[here], gathered(c).at[there]
        if hop == HY:
            rows = pl.ds(way * HALF, HALF)
            src, dst = src.at[rows], dst.at[rows]
        return send(src, dst, ys.at[c, hop - 1, way], yr.at[c, hop - 1, way], at(y + 1 - 2 * way, x))

    def across(c, k):
        src, dst = picked(c, k), arrived(c, k)
        return send(src, dst, xs.at[c, k], xr.at[c, k], at(y, x + k))

    def picked(i, k):
        c, lo, hi = OUT[i]
        return sm.at[k] if c is None else sx.at[c, k, :, :, lo:hi]

    def arrived(i, k):
        c, lo, hi = OUT[i]
        return rm.at[:, k] if c is None else rx.at[c, :, k, :, lo:hi]

    def piece(a, home, tile):
        p = pl.multiple_of((lax.rem(home + 2 * NZ, NZ) * 2 + core) * SLICE, SLICE)
        j = slice(None) if tile is None else pl.ds(tile, 1)
        return win.at[j, pl.ds(p, SLICE), :] if a == 0 else wout.at[j, :, pl.ds(p, SLICE)]

    def weights(a, hop, way):
        part = piece(a, z - (hop - 1) * (1 - 2 * way), way if hop == HZ else None)
        return send(part, part, ws.at[a, hop - 1, way], wr.at[a, hop - 1, way], at_z(z + 1 - 2 * way, core))

    def twin(a, hop, way):
        part = piece(a, z - hop * (1 - 2 * way), way if hop == HZ else None)
        return send(part, part, cs.at[a, hop, way], cr.at[a, hop, way], at_z(z, 1 - core))

    barrier = pltpu.get_barrier_semaphore()
    others = partners()
    for other in others:
        pl.semaphore_signal(barrier, inc=1, device_id=other, device_id_type=MESH)

    own = []
    for c in range(2 * NCH):
        src = (tok if c < NCH else dy).at[:, pl.ds((c % NCH) * CHUNK, CHUNK)]
        own.append(pltpu.make_async_copy(src, xg.at[c, 0], near.at[c]))
    for a, src in ((0, w_in), (1, w_out)):
        own.append(pltpu.make_async_copy(src, piece(a, z, None), near.at[2 * NCH + a]))
    for copy in own:
        copy.start()
    mg[0] = token_table(columns(routes[...]), columns(gates[...]), tiles[...])
    pl.semaphore_wait(barrier, len(others))

    def pick(i, k):
        rows = dot(sel[k * 2 * ROWS : (k + 1) * 2 * ROWS, :], gathered(i)[...].reshape(ALL_TOK, -1), ((1,), (0,)))
        rows = rows.astype(BF16).reshape(TILES_DEV, ROWS, -1)
        if k == 0:
            arrived(i, 0)[...] = rows
        else:
            picked(i, k)[...] = rows
            across(i, k).start()

    def project(i):
        c, lo, hi = OUT[i]
        for k in range(1, NX):
            across(i, k).wait_recv()
        if c is None:
            return
        cols = slice(c % NCH * CHUNK + lo, c % NCH * CHUNK + hi)
        for j in range(TILES_DEV):
            rows = rx[c, j, :, :, lo:hi].reshape(ALL_ROWS, hi - lo)
            if c < NCH:
                value, total = dot(rows, win[j, cols, :], ((1,), (0,))), hidden
            else:
                value, total = dot(rows, wout[j, :, cols], ((1,), (1,))), back
            if c % NCH == 0 and lo == 0:
                total[j] = value
            else:
                total[j] += value

    tasks = []
    for s in range(STARTS[-1] + HY + LAG + 1):
        for i in range(len(OUT)):
            if s == STARTS[i]:
                if OUT[i][0] is not None and OUT[i][1] == 0:
                    own[OUT[i][0]].wait()
                for way in range(2):
                    ring(i, 1, way).start()
        moving = [i for i in range(len(OUT)) if 1 <= s - STARTS[i] <= HY]
        late = [i for i in range(len(OUT)) if s - STARTS[i] == HY + LAG]
        for i in moving if s <= HY + 2 else reversed(moving):
            hop = s - STARTS[i]
            for way in range(2):
                ring(i, hop, way).wait_recv()
                if hop < HY:
                    ring(i, hop + 1, way).start()
            if hop == HY:
                if i == 0:
                    fill_selection(mg[...].reshape(ALL_TOK, 128), sel)
                tasks += [(pick, i, k) for k in (2, 1, 3, 0)]
            for task in [tasks.pop(0) for _ in range(min(2, len(tasks)))]:
                task[0](*task[1:])
        if s < 6 or s >= STARTS[-3] + HY:
            for task in tasks:
                task[0](*task[1:])
            tasks = []
        if s % 2 == 0 and s <= 2 * HZ:
            hop = s // 2
            for a in range(2):
                if hop == 0:
                    own[2 * NCH + a].wait()
                for way in range(2):
                    if hop > 0:
                        weights(a, hop, way).wait_recv()
                    if hop > 0 or way == 0:
                        twin(a, hop, way).start()
                    if hop < HZ:
                        weights(a, hop + 1, way).start()
        if s == 2 * HZ + 1:
            for a in range(2):
                for hop in range(HZ + 1):
                    for way in range(2 if hop > 0 else 1):
                        twin(a, hop, way).wait_recv()
        tasks += [(project, i) for i in late]

    for task in tasks:
        task[0](*task[1:])

    def term(i, k):
        c, lo, hi = BACK[i]
        return gp.at[k] if c is None else sx.at[c, k, :, :, lo:hi]

    def landed_terms(i):
        c, lo, hi = BACK[i]
        return bm if c is None else bx.at[c, :, :, :, lo:hi]

    def return_x(i, k):
        return send(term(i, k), landed_terms(i).at[k], qs.at[i, k], qr.at[i, k], at(y, x - k))

    def partial(i):
        c, lo, hi = BACK[i]
        return pm if c is None else xg.at[c, :, :, lo:hi]

    def outgoing(i, hop, way):
        c, lo, hi = BACK[i]
        return om.at[hop - 1, way] if c is None else xg.at[NCH + c, (hop - 1) * 2 + way, :, lo:hi]

    def incoming(i, hop, way):
        c, lo, hi = BACK[i]
        return im.at[hop - 1, way] if c is None else ib.at[c, hop - 1, way, :, lo:hi]

    def return_y(c, hop, way):
        src, dst = outgoing(c, hop, way), incoming(c, hop, way)
        if hop == 1:
            rows = pl.ds(way * HALF, HALF)
            src, dst = src.at[rows], dst.at[rows]
        return send(src, dst, rs.at[c, hop - 1, way], rr.at[c, hop - 1, way], at(y - 1 + 2 * way, x))

    def swap(a):
        src, dst = (parts_in, twin_in) if a == 0 else (parts_out, twin_out)
        return send(src.at[:, 1 - core], dst, ks.at[a], kr.at[a], at_z(z, 1 - core))

    def return_z(a, hop, way):
        src, dst = (zo_in, zi_in) if a == 0 else (zo_out, zi_out)
        src, dst = src.at[hop - 1, way], dst.at[hop - 1, way]
        if hop == 1:
            src, dst = src.at[pl.ds(way, 1)], dst.at[pl.ds(way, 1)]
        return send(src, dst, zs.at[a, hop - 1, way], zr.at[a, hop - 1, way], at_z(z - 1 + 2 * way, core))

    def chip_sum(a, slot, tile):
        home = lax.rem(z - slot + NZ, NZ)
        mine, other = (parts_in, twin_in) if a == 0 else (parts_out, twin_out)
        return mine[home, core, tile].astype(F32) + other[home, tile].astype(F32)

    lane = iota((ALL_ROWS, 128), 1)
    for j in range(TILES_DEV):
        tile = e * TILES_DEV + j
        table = rm[j].reshape(ALL_ROWS, 128).astype(F32)
        gate = jnp.sum(jnp.where(lane == TILES + tile, table, 0.0), axis=1, keepdims=True)
        act, slope = gelu_pair(hidden[j])
        gate_part = jnp.sum(act * back[j], axis=1, keepdims=True)
        terms = jnp.where(lane == tile, gate_part, 0.0).astype(BF16).reshape(NX, ROWS, 128)
        bm[0, j] = terms[0]
        for k in range(1, NX):
            gp[k, j] = terms[k]
        gh[j] = (gate * back[j] * slope).astype(BF16)
        ga[j] = (gate * act).astype(BF16)

    def set_out(i):
        c, lo, hi = BACK[i]
        if c is not None:
            cols = slice(c * CHUNK + lo, c * CHUNK + hi)
            for j in range(TILES_DEV):
                rows = dot(gh[j], win[j, cols, :], ((1,), (1,))).astype(BF16).reshape(NX, ROWS, hi - lo)
                landed_terms(i)[0, j] = rows[0]
                for k in range(1, NX):
                    term(i, k)[j] = rows[k]
        for k in (2, 1, 3):
            return_x(i, k).start()

    for i in range(len(OUT)):
        for k in range(1, NX):
            across(i, k).wait_send()
    for i in range(AHEAD):
        set_out(i)

    def tile_terms(a, c):
        for j in range(TILES_DEV):
            rows = rx[a * NCH + c, j].reshape(ALL_ROWS, CHUNK)
            part = (dot(ga[j], rows, ((0,), (0,))) if a else dot(rows, gh[j], ((0,), (0,)))).astype(BF16)
            for i in range(CHUNK // SLICE):
                q = c * (CHUNK // SLICE) + i
                cols = slice(i * SLICE, (i + 1) * SLICE)
                if a:
                    parts_out[q // 2, q % 2, j] = part[:, cols]
                else:
                    parts_in[q // 2, q % 2, j] = part[cols, :]

    for c in range(len(OUT)):
        for hop in range(1, HY + 1):
            for way in range(2):
                ring(c, hop, way).wait_send()

    for s in range(RETURNS[-1] + HY + 1):
        for c in range(len(BACK)):
            hop = s - RETURNS[c]
            if 1 <= hop < HY:
                for way in range(2):
                    return_y(c, hop, way).wait_recv()
                    slot = HY - hop if way == 0 else HY + hop
                    if hop == 1:
                        rows = slice(way * HALF, (way + 1) * HALF)
                        rest = slice((1 - way) * HALF, (2 - way) * HALF)
                        outgoing(c, 2, way)[rows] = (
                            partial(c)[slot, rows].astype(F32) + incoming(c, 1, way)[rows].astype(F32)
                        ).astype(BF16)
                        outgoing(c, 2, way)[rest] = partial(c)[slot, rest]
                    else:
                        outgoing(c, hop + 1, way)[...] = (
                            partial(c)[slot].astype(F32) + incoming(c, hop, way)[...].astype(F32)
                        ).astype(BF16)
                    return_y(c, hop + 1, way).start()
            if hop == HY:
                total = partial(c)[0].astype(F32)
                for way in range(2):
                    return_y(c, hop, way).wait_recv()
                    total += incoming(c, hop, way)[...].astype(F32)
                if BACK[c][0] is None:
                    of_tile = jnp.where(iota((TOK, 128), 1) < TILES, tile_experts(tiles[...]), -1.0)
                    cols = columns(routes[...])
                    ones = jnp.ones((8, 128), BF16)
                    for k in range(routes.shape[0]):
                        mine = jnp.where(cols[:, k : k + 1] == of_tile, total, 0.0).astype(BF16)
                        gg[k : k + 1, :] = dot(ones, mine, ((1,), (1,)))[0:1, :]
                else:
                    gt[:, BACK[c][0] * CHUNK + BACK[c][1] : BACK[c][0] * CHUNK + BACK[c][2]] = total.astype(BF16)
        for a in range(2):
            if s == 4:
                swap(a).wait_recv()
                for way in range(2):
                    (zo_in if a == 0 else zo_out)[0, way, way] = chip_sum(a, HZ, way).astype(BF16)
                    return_z(a, 1, way).start()
            hop = s - 4
            if 1 <= hop < HZ:
                stage, landed = (zo_in, zi_in) if a == 0 else (zo_out, zi_out)
                for way in range(2):
                    return_z(a, hop, way).wait_recv()
                    slot = HZ - hop if way == 0 else HZ + hop
                    for tile in range(TILES_DEV):
                        value = chip_sum(a, slot, tile)
                        if hop > 1 or tile == way:
                            value += landed[hop - 1, way, tile].astype(F32)
                        stage[hop, way, tile] = value.astype(BF16)
                    return_z(a, hop + 1, way).start()
            if hop == HZ:
                landed = zi_in if a == 0 else zi_out
                for way in range(2):
                    return_z(a, HZ, way).wait_recv()
                for tile in range(TILES_DEV):
                    value = chip_sum(a, 0, tile)
                    for way in range(2):
                        value += landed[HZ - 1, way, tile].astype(F32)
                    (gin if a == 0 else gout)[tile] = value
        if s in RETURNS:
            c = RETURNS.index(s)
            if c + AHEAD < len(BACK):
                set_out(c + AHEAD)
            for k in range(1, NX):
                return_x(c, k).wait_recv()
            rows = landed_terms(c)[...].reshape(SEL, -1)
            partial(c)[...] = dot(sel[...], rows, ((0,), (0,))).astype(BF16).reshape(NY, TOK, -1)
            for way in range(2):
                rows = slice(way * HALF, (way + 1) * HALF)
                outgoing(c, 1, way)[rows] = partial(c)[HY, rows]
                return_y(c, 1, way).start()
        if s < 4:
            for c in (0, 1) if s % 2 == 0 else (2, 3):
                tile_terms(s // 2, c)
        for a in range(2):
            if s == 2 * a + 1:
                swap(a).start()

    for c in range(len(BACK)):
        for k in range(1, NX):
            return_x(c, k).wait_send()
        for hop in range(1, HY + 1):
            for way in range(2):
                return_y(c, hop, way).wait_send()
    for a in range(2):
        swap(a).wait_send()
        for hop in range(HZ + 1):
            for way in range(2):
                if hop > 0 or way == 0:
                    twin(a, hop, way).wait_send()
                if hop > 0:
                    weights(a, hop, way).wait_send()
                    return_z(a, hop, way).wait_send()


def layer(tokens, grad_out, routes, gates, tiles, w_in, w_out):
    vmem, anywhere = pl.BlockSpec(memory_space=pltpu.VMEM), pl.BlockSpec(memory_space=pl.ANY)
    dma = pltpu.SemaphoreType.DMA

    def hold(*shape):
        return pltpu.VMEM(shape, BF16)

    return pl.pallas_call(
        layer_kernel,
        out_shape=(
            jax.ShapeDtypeStruct((TOK, D), BF16),
            jax.ShapeDtypeStruct(routes.shape, F32),
            jax.ShapeDtypeStruct(w_in.shape, F32),
            jax.ShapeDtypeStruct(w_out.shape, F32),
        ),
        in_specs=[anywhere, anywhere, vmem, vmem, vmem, anywhere, anywhere],
        out_specs=(vmem,) * 4,
        scratch_shapes=[
            hold(2 * NCH, NY, TOK, CHUNK),
            hold(NY, TOK, 128),
            hold(2 * NCH, NX, TILES_DEV, ROWS, CHUNK),
            hold(NX, TILES_DEV, ROWS, 128),
            hold(2 * NCH, TILES_DEV, NX, ROWS, CHUNK),
            hold(TILES_DEV, NX, ROWS, 128),
            hold(SEL, ALL_TOK),
            hold(TILES_DEV, D, TILE),
            hold(TILES_DEV, TILE, D),
            pltpu.VMEM((TILES_DEV, ALL_ROWS, TILE), F32),
            pltpu.VMEM((TILES_DEV, ALL_ROWS, TILE), F32),
            hold(TILES_DEV, ALL_ROWS, TILE),
            hold(TILES_DEV, ALL_ROWS, TILE),
            hold(NX, TILES_DEV, ROWS, 128),
            hold(NCH, NX, TILES_DEV, ROWS, CHUNK),
            hold(NX, TILES_DEV, ROWS, 128),
            hold(NY, TOK, 128),
            hold(HY, 2, TOK, 128),
            hold(NCH, HY, 2, TOK, CHUNK),
            hold(HY, 2, TOK, 128),
            hold(NZ, 2, TILES_DEV, SLICE, TILE),
            hold(NZ, 2, TILES_DEV, TILE, SLICE),
            hold(NZ, TILES_DEV, SLICE, TILE),
            hold(NZ, TILES_DEV, TILE, SLICE),
            hold(HZ, 2, TILES_DEV, SLICE, TILE),
            hold(HZ, 2, TILES_DEV, SLICE, TILE),
            hold(HZ, 2, TILES_DEV, TILE, SLICE),
            hold(HZ, 2, TILES_DEV, TILE, SLICE),
            dma((2 * NCH + 2,)),
            dma((len(OUT), HY, 2)),
            dma((len(OUT), HY, 2)),
            dma((len(OUT), NX)),
            dma((len(OUT), NX)),
            dma((2, HZ, 2)),
            dma((2, HZ, 2)),
            dma((2, HZ + 1, 2)),
            dma((2, HZ + 1, 2)),
            dma((len(BACK), NX)),
            dma((len(BACK), NX)),
            dma((len(BACK), HY, 2)),
            dma((len(BACK), HY, 2)),
            dma((2,)),
            dma((2,)),
            dma((2, HZ, 2)),
            dma((2, HZ, 2)),
        ],
        compiler_params=pltpu.CompilerParams(
            collective_id=0, has_side_effects=True, vmem_limit_bytes=60 << 20
        ),
        name="layer",
    )(tokens, grad_out, routes, gates, tiles, w_in, w_out)


def finish_kernel(*refs):
    n = len(refs) // 2
    for i in range(n):
        refs[n + i][...] = refs[i][...]


def finish(*arrays):
    vmem = pl.BlockSpec(memory_space=pltpu.VMEM)
    return pl.pallas_call(
        finish_kernel,
        out_shape=tuple(jax.ShapeDtypeStruct(a.shape, a.dtype) for a in arrays),
        in_specs=[vmem] * len(arrays),
        out_specs=(vmem,) * len(arrays),
        name="finish",
    )(*arrays)


def on_device(tokens, grad_out, routes, gates, expert_tiles, w_in, w_out):
    results = layer(tokens, grad_out, routes.T, gates.T, expert_tiles.reshape(1, -1), w_in, w_out)
    grad_tokens, gates_rows, grad_in, grad_out_w = finish(*results)
    return grad_tokens, gates_rows.T, grad_in, grad_out_w


def solution(mesh):
    rows = P(("dp", "expert"), None)
    w_in, w_out = P("expert", "dp", None), P("expert", None, "dp")
    return jax.shard_map(
        on_device,
        mesh=mesh,
        in_specs=(rows, rows, rows, rows, P(), w_in, w_out),
        out_specs=(rows, rows, w_in, w_out),
        check_vma=False,
    )
```

```python
import jax
import jax.numpy as jnp
from jax import lax
from jax.experimental import pallas as pl
from jax.experimental.pallas import tpu as pltpu
from jax.sharding import PartitionSpec as P

MESH = pl.DeviceIdType.MESH
BF16, F32 = jnp.bfloat16, jnp.float32

NY, NX = 8, 4
TOK = 128
D, TILE = 2048, 256
TILES, TILES_DEV = 64, 2
MOST = 13
CHUNK = 512
NCH = D // CHUNK
ROWS = 112
SEL = NX * TILES_DEV * ROWS
ALL_TOK = NY * TOK
NZ = 8
SLICE = D // (2 * NZ)
HALF = TOK // 2


def my_place():
    e, p = lax.axis_index("expert"), lax.axis_index("dp")
    return e // NX, e % NX, p // 2, p % 2


def at(y, x):
    return {"expert": lax.rem(y + NY, NY) * NX + lax.rem(x + NX, NX)}


def at_z(z, core):
    return {"dp": lax.rem(z + NZ, NZ) * 2 + core}


def partners():
    y, x, z, core = my_place()
    others = [at(y + 1, x), at(y - 1, x)] + [at(y, x + k) for k in range(1, NX)]
    others += [at_z(z + 1, core), at_z(z - 1, core), at_z(z, 1 - core)]
    return others


def dot(a, b, dims):
    return lax.dot_general(a, b, (dims, ((), ())), preferred_element_type=F32)


def send(src, dst, send_sem, recv_sem, to):
    return pltpu.make_async_remote_copy(
        src_ref=src, dst_ref=dst, send_sem=send_sem, recv_sem=recv_sem, device_id=to, device_id_type=MESH
    )


def iota(shape, dim):
    return lax.broadcasted_iota(jnp.int32, shape, dim)


def columns(rows):
    eye = jnp.where(iota((TOK, TOK), 0) == iota((TOK, TOK), 1), 1.0, 0.0).astype(BF16)
    return dot(eye, rows.astype(F32).astype(BF16), ((1,), (1,)))


def tile_experts(tiles):
    n = tiles.shape[1]
    upto = iota((n, n), 1) <= iota((n, n), 0)
    ends = jnp.sum(jnp.where(upto, tiles.astype(F32), 0.0), axis=1, keepdims=True)
    lane = iota((n, 128), 1) % TILES
    return jnp.sum(jnp.where(ends <= lane.astype(F32), 1.0, 0.0), axis=0, keepdims=True)


def token_table(routes, gates, tiles):
    of_tile = tile_experts(tiles)
    named = jnp.zeros((TOK, 128), F32)
    gate = jnp.zeros((TOK, 128), F32)
    for k in range(routes.shape[1]):
        hit = routes[:, k : k + 1] == of_tile
        named = jnp.where(hit, 1.0, named)
        gate = jnp.where(hit, gates[:, k : k + 1], gate)
    upto = iota((TOK, TOK), 1) <= iota((TOK, TOK), 0)
    rank = dot(jnp.where(upto, 1.0, 0.0).astype(BF16), named.astype(BF16), ((1,), (0,)))
    slot = jnp.where(named > 0.0, rank - 1.0, -1.0)
    return jnp.where(iota((TOK, 128), 1) < TILES, slot, gate).astype(BF16)


def fill_selection(table, sel):
    y, x, _, _ = my_place()
    a = iota((8, 128), 0)
    want = (y * NX + lax.rem(x + a // TILES_DEV, NX)) * TILES_DEV + a % TILES_DEV
    pick = jnp.where(iota((8, 128), 1) == want, 1.0, 0.0).astype(BF16)
    slots = dot(pick, table, ((1,), (1,)))
    source = iota((8, ALL_TOK), 1) // TOK
    place = jnp.where(slots >= 0.0, slots + (source * MOST).astype(F32), -1.0)
    row = iota((ROWS, ALL_TOK), 0).astype(F32)
    for a in range(NX * TILES_DEV):
        sel[a * ROWS : (a + 1) * ROWS, :] = jnp.where(place[a : a + 1, :] == row, 1.0, 0.0).astype(BF16)


def gelu_pair(v):
    t = jnp.tanh(0.7978845608 * (v + 0.044715 * v * v * v))
    act = 0.5 * v * (1.0 + t)
    slope = 0.5 * (1.0 + t) + 0.5 * v * (1.0 - t * t) * (0.7978845608 * (1.0 + 3.0 * 0.044715 * v * v))
    return act, slope


OUT = [(None, 0, 128), (0, 0, 256), (0, 256, 512)] + [(c, 0, CHUNK) for c in range(1, 2 * NCH - 1)]
OUT += [(2 * NCH - 1, 0, 256), (2 * NCH - 1, 256, 512)]
STARTS = [0, 0, 1, 3, 5, 7, 9, 11, 13, 15, 16]
LAG = 6
BACK = [(None, 0, 128)] + [(c, 0, CHUNK) for c in range(NCH)]
RETURNS = list(range(len(BACK)))
AHEAD = 2
HY, HZ = NY // 2, NZ // 2
ALL_ROWS = NX * ROWS


def layer_kernel(
    tok, dy, routes, gates, tiles, w_in, w_out,
    gt, gg, gin, gout,
    xg, mg, sx, sm, rx, rm, sel, win, wout, hidden, back, gh, ga,
    gp, bx, bm, pm, om, ib, im, parts_in, parts_out, twin_in, twin_out, zo_in, zi_in, zo_out, zi_out,
    near, ys, yr, xs, xr, ws, wr, cs, cr, qs, qr, rs, rr, ks, kr, zs, zr,
):
    y, x, z, core = my_place()
    e = lax.axis_index("expert")

    def gathered(i):
        c, lo, hi = OUT[i]
        return mg if c is None else xg.at[c, :, :, lo:hi]

    def ring(c, hop, way):
        here = hop - 1 if way == 0 else (NY - (hop - 1)) % NY
        there = hop if way == 0 else NY - hop
        src, dst = gathered(c).at[here], gathered(c).at[there]
        if hop == HY:
            rows = pl.ds(way * HALF, HALF)
            src, dst = src.at[rows], dst.at[rows]
        return send(src, dst, ys.at[c, hop - 1, way], yr.at[c, hop - 1, way], at(y + 1 - 2 * way, x))

    def across(c, k):
        src, dst = picked(c, k), arrived(c, k)
        return send(src, dst, xs.at[c, k], xr.at[c, k], at(y, x + k))

    def picked(i, k):
        c, lo, hi = OUT[i]
        return sm.at[k] if c is None else sx.at[c, k, :, :, lo:hi]

    def arrived(i, k):
        c, lo, hi = OUT[i]
        return rm.at[:, k] if c is None else rx.at[c, :, k, :, lo:hi]

    def piece(a, home, tile):
        p = pl.multiple_of((lax.rem(home + 2 * NZ, NZ) * 2 + core) * SLICE, SLICE)
        j = slice(None) if tile is None else pl.ds(tile, 1)
        return win.at[j, pl.ds(p, SLICE), :] if a == 0 else wout.at[j, :, pl.ds(p, SLICE)]

    def weights(a, hop, way):
        part = piece(a, z - (hop - 1) * (1 - 2 * way), way if hop == HZ else None)
        return send(part, part, ws.at[a, hop - 1, way], wr.at[a, hop - 1, way], at_z(z + 1 - 2 * way, core))

    def twin(a, hop, way):
        part = piece(a, z - hop * (1 - 2 * way), way if hop == HZ else None)
        return send(part, part, cs.at[a, hop, way], cr.at[a, hop, way], at_z(z, 1 - core))

    barrier = pltpu.get_barrier_semaphore()
    others = partners()
    for other in others:
        pl.semaphore_signal(barrier, inc=1, device_id=other, device_id_type=MESH)

    own = []
    for c in range(2 * NCH):
        src = (tok if c < NCH else dy).at[:, pl.ds((c % NCH) * CHUNK, CHUNK)]
        own.append(pltpu.make_async_copy(src, xg.at[c, 0], near.at[c]))
    for a, src in ((0, w_in), (1, w_out)):
        own.append(pltpu.make_async_copy(src, piece(a, z, None), near.at[2 * NCH + a]))
    for copy in own:
        copy.start()
    mg[0] = token_table(columns(routes[...]), columns(gates[...]), tiles[...])
    pl.semaphore_wait(barrier, len(others))

    def pick(i, k):
        rows = dot(sel[k * 2 * ROWS : (k + 1) * 2 * ROWS, :], gathered(i)[...].reshape(ALL_TOK, -1), ((1,), (0,)))
        rows = rows.astype(BF16).reshape(TILES_DEV, ROWS, -1)
        if k == 0:
            arrived(i, 0)[...] = rows
        else:
            picked(i, k)[...] = rows
            across(i, k).start()

    def project(i):
        c, lo, hi = OUT[i]
        for k in range(1, NX):
            across(i, k).wait_recv()
        if c is None:
            return
        cols = slice(c % NCH * CHUNK + lo, c % NCH * CHUNK + hi)
        for j in range(TILES_DEV):
            rows = rx[c, j, :, :, lo:hi].reshape(ALL_ROWS, hi - lo)
            if c < NCH:
                value, total = dot(rows, win[j, cols, :], ((1,), (0,))), hidden
            else:
                value, total = dot(rows, wout[j, :, cols], ((1,), (1,))), back
            if c % NCH == 0 and lo == 0:
                total[j] = value
            else:
                total[j] += value

    tasks = []
    for s in range(STARTS[-1] + HY + LAG + 1):
        for i in range(len(OUT)):
            if s == STARTS[i]:
                if OUT[i][0] is not None and OUT[i][1] == 0:
                    own[OUT[i][0]].wait()
                for way in range(2):
                    ring(i, 1, way).start()
        moving = [i for i in range(len(OUT)) if 1 <= s - STARTS[i] <= HY]
        late = [i for i in range(len(OUT)) if s - STARTS[i] == HY + LAG]
        for i in moving if s <= HY + 2 else reversed(moving):
            hop = s - STARTS[i]
            for way in range(2):
                ring(i, hop, way).wait_recv()
                if hop < HY:
                    ring(i, hop + 1, way).start()
            if hop == HY:
                if i == 0:
                    fill_selection(mg[...].reshape(ALL_TOK, 128), sel)
                tasks += [(pick, i, k) for k in (2, 1, 3, 0)]
            for task in [tasks.pop(0) for _ in range(min(2, len(tasks)))]:
                task[0](*task[1:])
        if s < 6 or s >= STARTS[-3] + HY:
            for task in tasks:
                task[0](*task[1:])
            tasks = []
        if s % 2 == 0 and s <= 2 * HZ:
            hop = s // 2
            for a in range(2):
                if hop == 0:
                    own[2 * NCH + a].wait()
                for way in range(2):
                    if hop > 0:
                        weights(a, hop, way).wait_recv()
                    if hop > 0 or way == 0:
                        twin(a, hop, way).start()
                    if hop < HZ:
                        weights(a, hop + 1, way).start()
        if s == 2 * HZ + 1:
            for a in range(2):
                for hop in range(HZ + 1):
                    for way in range(2 if hop > 0 else 1):
                        twin(a, hop, way).wait_recv()
        tasks += [(project, i) for i in late]

    for task in tasks:
        task[0](*task[1:])

    def term(i, k):
        c, lo, hi = BACK[i]
        return gp.at[k] if c is None else sx.at[c, k, :, :, lo:hi]

    def landed_terms(i):
        c, lo, hi = BACK[i]
        return bm if c is None else bx.at[c, :, :, :, lo:hi]

    def return_x(i, k):
        return send(term(i, k), landed_terms(i).at[k], qs.at[i, k], qr.at[i, k], at(y, x - k))

    def partial(i):
        c, lo, hi = BACK[i]
        return pm if c is None else xg.at[c, :, :, lo:hi]

    def outgoing(i, hop, way):
        c, lo, hi = BACK[i]
        return om.at[hop - 1, way] if c is None else xg.at[NCH + c, (hop - 1) * 2 + way, :, lo:hi]

    def incoming(i, hop, way):
        c, lo, hi = BACK[i]
        return im.at[hop - 1, way] if c is None else ib.at[c, hop - 1, way, :, lo:hi]

    def return_y(c, hop, way):
        src, dst = outgoing(c, hop, way), incoming(c, hop, way)
        if hop == 1:
            rows = pl.ds(way * HALF, HALF)
            src, dst = src.at[rows], dst.at[rows]
        return send(src, dst, rs.at[c, hop - 1, way], rr.at[c, hop - 1, way], at(y - 1 + 2 * way, x))

    def swap(a):
        src, dst = (parts_in, twin_in) if a == 0 else (parts_out, twin_out)
        return send(src.at[:, 1 - core], dst, ks.at[a], kr.at[a], at_z(z, 1 - core))

    def return_z(a, hop, way):
        src, dst = (zo_in, zi_in) if a == 0 else (zo_out, zi_out)
        src, dst = src.at[hop - 1, way], dst.at[hop - 1, way]
        if hop == 1:
            src, dst = src.at[pl.ds(way, 1)], dst.at[pl.ds(way, 1)]
        return send(src, dst, zs.at[a, hop - 1, way], zr.at[a, hop - 1, way], at_z(z - 1 + 2 * way, core))

    def chip_sum(a, slot, tile):
        home = lax.rem(z - slot + NZ, NZ)
        mine, other = (parts_in, twin_in) if a == 0 else (parts_out, twin_out)
        return mine[home, core, tile].astype(F32) + other[home, tile].astype(F32)

    lane = iota((ALL_ROWS, 128), 1)
    for j in range(TILES_DEV):
        tile = e * TILES_DEV + j
        table = rm[j].reshape(ALL_ROWS, 128).astype(F32)
        gate = jnp.sum(jnp.where(lane == TILES + tile, table, 0.0), axis=1, keepdims=True)
        act, slope = gelu_pair(hidden[j])
        gate_part = jnp.sum(act * back[j], axis=1, keepdims=True)
        terms = jnp.where(lane == tile, gate_part, 0.0).astype(BF16).reshape(NX, ROWS, 128)
        bm[0, j] = terms[0]
        for k in range(1, NX):
            gp[k, j] = terms[k]
        gh[j] = (gate * back[j] * slope).astype(BF16)
        ga[j] = (gate * act).astype(BF16)

    def set_out(i):
        c, lo, hi = BACK[i]
        if c is not None:
            cols = slice(c * CHUNK + lo, c * CHUNK + hi)
            for j in range(TILES_DEV):
                rows = dot(gh[j], win[j, cols, :], ((1,), (1,))).astype(BF16).reshape(NX, ROWS, hi - lo)
                landed_terms(i)[0, j] = rows[0]
                for k in range(1, NX):
                    term(i, k)[j] = rows[k]
        for k in (2, 1, 3):
            return_x(i, k).start()

    for i in range(len(OUT)):
        for k in range(1, NX):
            across(i, k).wait_send()
    for i in range(AHEAD):
        set_out(i)

    def tile_terms(a, c):
        for j in range(TILES_DEV):
            rows = rx[a * NCH + c, j].reshape(ALL_ROWS, CHUNK)
            part = (dot(ga[j], rows, ((0,), (0,))) if a else dot(rows, gh[j], ((0,), (0,)))).astype(BF16)
            for i in range(CHUNK // SLICE):
                q = c * (CHUNK // SLICE) + i
                cols = slice(i * SLICE, (i + 1) * SLICE)
                if a:
                    parts_out[q // 2, q % 2, j] = part[:, cols]
                else:
                    parts_in[q // 2, q % 2, j] = part[cols, :]

    for a in range(2):
        for c in range(NCH):
            tile_terms(a, c)
        swap(a).start()
    for c in range(len(OUT)):
        for hop in range(1, HY + 1):
            for way in range(2):
                ring(c, hop, way).wait_send()

    for s in range(RETURNS[-1] + HY + 1):
        for c in range(len(BACK)):
            hop = s - RETURNS[c]
            if 1 <= hop < HY:
                for way in range(2):
                    return_y(c, hop, way).wait_recv()
                    slot = HY - hop if way == 0 else HY + hop
                    if hop == 1:
                        rows = slice(way * HALF, (way + 1) * HALF)
                        rest = slice((1 - way) * HALF, (2 - way) * HALF)
                        outgoing(c, 2, way)[rows] = (
                            partial(c)[slot, rows].astype(F32) + incoming(c, 1, way)[rows].astype(F32)
                        ).astype(BF16)
                        outgoing(c, 2, way)[rest] = partial(c)[slot, rest]
                    else:
                        outgoing(c, hop + 1, way)[...] = (
                            partial(c)[slot].astype(F32) + incoming(c, hop, way)[...].astype(F32)
                        ).astype(BF16)
                    return_y(c, hop + 1, way).start()
            if hop == HY:
                total = partial(c)[0].astype(F32)
                for way in range(2):
                    return_y(c, hop, way).wait_recv()
                    total += incoming(c, hop, way)[...].astype(F32)
                if BACK[c][0] is None:
                    of_tile = jnp.where(iota((TOK, 128), 1) < TILES, tile_experts(tiles[...]), -1.0)
                    cols = columns(routes[...])
                    ones = jnp.ones((8, 128), BF16)
                    for k in range(routes.shape[0]):
                        mine = jnp.where(cols[:, k : k + 1] == of_tile, total, 0.0).astype(BF16)
                        gg[k : k + 1, :] = dot(ones, mine, ((1,), (1,)))[0:1, :]
                else:
                    gt[:, BACK[c][0] * CHUNK + BACK[c][1] : BACK[c][0] * CHUNK + BACK[c][2]] = total.astype(BF16)
        for a in range(2):
            if s == 1:
                swap(a).wait_recv()
                for way in range(2):
                    (zo_in if a == 0 else zo_out)[0, way, way] = chip_sum(a, HZ, way).astype(BF16)
                    return_z(a, 1, way).start()
            hop = s - 1
            if 1 <= hop < HZ:
                stage, landed = (zo_in, zi_in) if a == 0 else (zo_out, zi_out)
                for way in range(2):
                    return_z(a, hop, way).wait_recv()
                    slot = HZ - hop if way == 0 else HZ + hop
                    for tile in range(TILES_DEV):
                        value = chip_sum(a, slot, tile)
                        if hop > 1 or tile == way:
                            value += landed[hop - 1, way, tile].astype(F32)
                        stage[hop, way, tile] = value.astype(BF16)
                    return_z(a, hop + 1, way).start()
            if hop == HZ:
                landed = zi_in if a == 0 else zi_out
                for way in range(2):
                    return_z(a, HZ, way).wait_recv()
                for tile in range(TILES_DEV):
                    value = chip_sum(a, 0, tile)
                    for way in range(2):
                        value += landed[HZ - 1, way, tile].astype(F32)
                    (gin if a == 0 else gout)[tile] = value
        if s in RETURNS:
            c = RETURNS.index(s)
            if c + AHEAD < len(BACK):
                set_out(c + AHEAD)
            for k in range(1, NX):
                return_x(c, k).wait_recv()
            rows = landed_terms(c)[...].reshape(SEL, -1)
            partial(c)[...] = dot(sel[...], rows, ((0,), (0,))).astype(BF16).reshape(NY, TOK, -1)
            for way in range(2):
                rows = slice(way * HALF, (way + 1) * HALF)
                outgoing(c, 1, way)[rows] = partial(c)[HY, rows]
                return_y(c, 1, way).start()

    for c in range(len(BACK)):
        for k in range(1, NX):
            return_x(c, k).wait_send()
        for hop in range(1, HY + 1):
            for way in range(2):
                return_y(c, hop, way).wait_send()
    for a in range(2):
        swap(a).wait_send()
        for hop in range(HZ + 1):
            for way in range(2):
                if hop > 0 or way == 0:
                    twin(a, hop, way).wait_send()
                if hop > 0:
                    weights(a, hop, way).wait_send()
                    return_z(a, hop, way).wait_send()


def layer(tokens, grad_out, routes, gates, tiles, w_in, w_out):
    vmem, anywhere = pl.BlockSpec(memory_space=pltpu.VMEM), pl.BlockSpec(memory_space=pl.ANY)
    dma = pltpu.SemaphoreType.DMA

    def hold(*shape):
        return pltpu.VMEM(shape, BF16)

    return pl.pallas_call(
        layer_kernel,
        out_shape=(
            jax.ShapeDtypeStruct((TOK, D), BF16),
            jax.ShapeDtypeStruct(routes.shape, F32),
            jax.ShapeDtypeStruct(w_in.shape, F32),
            jax.ShapeDtypeStruct(w_out.shape, F32),
        ),
        in_specs=[anywhere, anywhere, vmem, vmem, vmem, anywhere, anywhere],
        out_specs=(vmem,) * 4,
        scratch_shapes=[
            hold(2 * NCH, NY, TOK, CHUNK),
            hold(NY, TOK, 128),
            hold(2 * NCH, NX, TILES_DEV, ROWS, CHUNK),
            hold(NX, TILES_DEV, ROWS, 128),
            hold(2 * NCH, TILES_DEV, NX, ROWS, CHUNK),
            hold(TILES_DEV, NX, ROWS, 128),
            hold(SEL, ALL_TOK),
            hold(TILES_DEV, D, TILE),
            hold(TILES_DEV, TILE, D),
            pltpu.VMEM((TILES_DEV, ALL_ROWS, TILE), F32),
            pltpu.VMEM((TILES_DEV, ALL_ROWS, TILE), F32),
            hold(TILES_DEV, ALL_ROWS, TILE),
            hold(TILES_DEV, ALL_ROWS, TILE),
            hold(NX, TILES_DEV, ROWS, 128),
            hold(NCH, NX, TILES_DEV, ROWS, CHUNK),
            hold(NX, TILES_DEV, ROWS, 128),
            hold(NY, TOK, 128),
            hold(HY, 2, TOK, 128),
            hold(NCH, HY, 2, TOK, CHUNK),
            hold(HY, 2, TOK, 128),
            hold(NZ, 2, TILES_DEV, SLICE, TILE),
            hold(NZ, 2, TILES_DEV, TILE, SLICE),
            hold(NZ, TILES_DEV, SLICE, TILE),
            hold(NZ, TILES_DEV, TILE, SLICE),
            hold(HZ, 2, TILES_DEV, SLICE, TILE),
            hold(HZ, 2, TILES_DEV, SLICE, TILE),
            hold(HZ, 2, TILES_DEV, TILE, SLICE),
            hold(HZ, 2, TILES_DEV, TILE, SLICE),
            dma((2 * NCH + 2,)),
            dma((len(OUT), HY, 2)),
            dma((len(OUT), HY, 2)),
            dma((len(OUT), NX)),
            dma((len(OUT), NX)),
            dma((2, HZ, 2)),
            dma((2, HZ, 2)),
            dma((2, HZ + 1, 2)),
            dma((2, HZ + 1, 2)),
            dma((len(BACK), NX)),
            dma((len(BACK), NX)),
            dma((len(BACK), HY, 2)),
            dma((len(BACK), HY, 2)),
            dma((2,)),
            dma((2,)),
            dma((2, HZ, 2)),
            dma((2, HZ, 2)),
        ],
        compiler_params=pltpu.CompilerParams(
            collective_id=0, has_side_effects=True, vmem_limit_bytes=60 << 20
        ),
        name="layer",
    )(tokens, grad_out, routes, gates, tiles, w_in, w_out)


def finish_kernel(*refs):
    n = len(refs) // 2
    for i in range(n):
        refs[n + i][...] = refs[i][...]


def finish(*arrays):
    vmem = pl.BlockSpec(memory_space=pltpu.VMEM)
    return pl.pallas_call(
        finish_kernel,
        out_shape=tuple(jax.ShapeDtypeStruct(a.shape, a.dtype) for a in arrays),
        in_specs=[vmem] * len(arrays),
        out_specs=(vmem,) * len(arrays),
        name="finish",
    )(*arrays)


def on_device(tokens, grad_out, routes, gates, expert_tiles, w_in, w_out):
    results = layer(tokens, grad_out, routes.T, gates.T, expert_tiles.reshape(1, -1), w_in, w_out)
    grad_tokens, gates_rows, grad_in, grad_out_w = finish(*results)
    return grad_tokens, gates_rows.T, grad_in, grad_out_w


def solution(mesh):
    rows = P(("dp", "expert"), None)
    w_in, w_out = P("expert", "dp", None), P("expert", None, "dp")
    return jax.shard_map(
        on_device,
        mesh=mesh,
        in_specs=(rows, rows, rows, rows, P(), w_in, w_out),
        out_specs=(rows, rows, w_in, w_out),
        check_vma=False,
    )
```

```python
import jax
import jax.numpy as jnp
from jax import lax
from jax.experimental import pallas as pl
from jax.experimental.pallas import tpu as pltpu
from jax.sharding import PartitionSpec as P

MESH = pl.DeviceIdType.MESH
BF16, F32 = jnp.bfloat16, jnp.float32

NY, NX = 8, 4
TOK = 128
D, TILE = 2048, 256
TILES, TILES_DEV = 64, 2
MOST = 13
CHUNK = 512
NCH = D // CHUNK
ONE = 8 * MOST
ROWS = TILES_DEV * ONE
SEL = NX * ROWS
ALL_TOK = NY * TOK
NZ = 8
SLICE = D // (2 * NZ)
HALF = TOK // 2


def my_place():
    e, p = lax.axis_index("expert"), lax.axis_index("dp")
    return e // NX, e % NX, p // 2, p % 2


def at(y, x):
    return {"expert": lax.rem(y + NY, NY) * NX + lax.rem(x + NX, NX)}


def at_z(z, core):
    return {"dp": lax.rem(z + NZ, NZ) * 2 + core}


def partners():
    y, x, z, core = my_place()
    others = [at(y + 1, x), at(y - 1, x)] + [at(y, x + k) for k in range(1, NX)]
    others += [at_z(z + 1, core), at_z(z - 1, core), at_z(z, 1 - core)]
    return others


def dot(a, b, dims):
    return lax.dot_general(a, b, (dims, ((), ())), preferred_element_type=F32)


def send(src, dst, send_sem, recv_sem, to):
    return pltpu.make_async_remote_copy(
        src_ref=src, dst_ref=dst, send_sem=send_sem, recv_sem=recv_sem, device_id=to, device_id_type=MESH
    )


def iota(shape, dim):
    return lax.broadcasted_iota(jnp.int32, shape, dim)


def columns(rows):
    eye = jnp.where(iota((TOK, TOK), 0) == iota((TOK, TOK), 1), 1.0, 0.0).astype(BF16)
    return dot(eye, rows.astype(F32).astype(BF16), ((1,), (1,)))


def tile_experts(tiles):
    n = tiles.shape[1]
    upto = iota((n, n), 1) <= iota((n, n), 0)
    ends = jnp.sum(jnp.where(upto, tiles.astype(F32), 0.0), axis=1, keepdims=True)
    lane = iota((n, 128), 1) % TILES
    return jnp.sum(jnp.where(ends <= lane.astype(F32), 1.0, 0.0), axis=0, keepdims=True)


def token_table(routes, gates, tiles):
    of_tile = tile_experts(tiles)
    named = jnp.zeros((TOK, 128), F32)
    gate = jnp.zeros((TOK, 128), F32)
    for k in range(routes.shape[1]):
        hit = routes[:, k : k + 1] == of_tile
        named = jnp.where(hit, 1.0, named)
        gate = jnp.where(hit, gates[:, k : k + 1], gate)
    upto = iota((TOK, TOK), 1) <= iota((TOK, TOK), 0)
    rank = dot(jnp.where(upto, 1.0, 0.0).astype(BF16), named.astype(BF16), ((1,), (0,)))
    slot = jnp.where(named > 0.0, rank - 1.0, -1.0)
    return jnp.where(iota((TOK, 128), 1) < TILES, slot, gate).astype(BF16)


def fill_selection(table, sel):
    y, x, _, _ = my_place()
    a = iota((8, 128), 0)
    want = (y * NX + lax.rem(x + a // TILES_DEV, NX)) * TILES_DEV + a % TILES_DEV
    pick = jnp.where(iota((8, 128), 1) == want, 1.0, 0.0).astype(BF16)
    slots = dot(pick, table, ((1,), (1,)))
    source = iota((8, ALL_TOK), 1) // TOK
    place = jnp.where(slots >= 0.0, slots + (source * MOST).astype(F32), -1000.0)
    row = iota((ROWS, ALL_TOK), 0).astype(F32)
    for k in range(NX):
        first, second = place[2 * k : 2 * k + 1, :], place[2 * k + 1 : 2 * k + 2, :] + float(ONE)
        sel[k * ROWS : (k + 1) * ROWS, :] = jnp.where((first == row) | (second == row), 1.0, 0.0).astype(BF16)


def gelu_pair(v):
    t = jnp.tanh(0.7978845608 * (v + 0.044715 * v * v * v))
    act = 0.5 * v * (1.0 + t)
    slope = 0.5 * (1.0 + t) + 0.5 * v * (1.0 - t * t) * (0.7978845608 * (1.0 + 3.0 * 0.044715 * v * v))
    return act, slope


OUT = [(None, 0, 128), (0, 0, 256), (0, 256, 512)] + [(c, 0, CHUNK) for c in range(1, 2 * NCH - 1)]
OUT += [(2 * NCH - 1, 0, 256), (2 * NCH - 1, 256, 512)]
STARTS = [0, 0, 1, 3, 5, 7, 9, 11, 13, 15, 16]
LAG = 6
BACK = [(None, 0, 128)] + [(c, 0, CHUNK) for c in range(NCH)]
RETURNS = list(range(len(BACK)))
AHEAD = 2
HY, HZ = NY // 2, NZ // 2


def layer_kernel(
    tok, dy, routes, gates, tiles, w_in, w_out,
    gt, gg, gin, gout,
    xg, mg, sx, sm, rx, rm, sel, win, wout, hidden, back, gh, ga,
    gp, bx, bm, pm, om, ib, im, parts_in, parts_out, twin_in, twin_out, zo_in, zi_in, zo_out, zi_out,
    near, ys, yr, xs, xr, ws, wr, cs, cr, qs, qr, rs, rr, ks, kr, zs, zr,
):
    y, x, z, core = my_place()
    e = lax.axis_index("expert")

    def gathered(i):
        c, lo, hi = OUT[i]
        return mg if c is None else xg.at[c, :, :, lo:hi]

    def ring(c, hop, way):
        here = hop - 1 if way == 0 else (NY - (hop - 1)) % NY
        there = hop if way == 0 else NY - hop
        src, dst = gathered(c).at[here], gathered(c).at[there]
        if hop == HY:
            rows = pl.ds(way * HALF, HALF)
            src, dst = src.at[rows], dst.at[rows]
        return send(src, dst, ys.at[c, hop - 1, way], yr.at[c, hop - 1, way], at(y + 1 - 2 * way, x))

    def across(c, k):
        src, dst = picked(c, k), arrived(c, k)
        return send(src, dst, xs.at[c, k], xr.at[c, k], at(y, x + k))

    def picked(i, k):
        c, lo, hi = OUT[i]
        return sm.at[k] if c is None else sx.at[c, k, :, lo:hi]

    def arrived(i, k):
        c, lo, hi = OUT[i]
        return rm.at[k] if c is None else rx.at[c, k, :, lo:hi]

    def piece(a, home, tile):
        p = pl.multiple_of((lax.rem(home + 2 * NZ, NZ) * 2 + core) * SLICE, SLICE)
        j = slice(None) if tile is None else pl.ds(tile, 1)
        return win.at[j, pl.ds(p, SLICE), :] if a == 0 else wout.at[j, :, pl.ds(p, SLICE)]

    def weights(a, hop, way):
        part = piece(a, z - (hop - 1) * (1 - 2 * way), way if hop == HZ else None)
        return send(part, part, ws.at[a, hop - 1, way], wr.at[a, hop - 1, way], at_z(z + 1 - 2 * way, core))

    def twin(a, hop, way):
        part = piece(a, z - hop * (1 - 2 * way), way if hop == HZ else None)
        return send(part, part, cs.at[a, hop, way], cr.at[a, hop, way], at_z(z, 1 - core))

    barrier = pltpu.get_barrier_semaphore()
    others = partners()
    for other in others:
        pl.semaphore_signal(barrier, inc=1, device_id=other, device_id_type=MESH)

    own = []
    for c in range(2 * NCH):
        src = (tok if c < NCH else dy).at[:, pl.ds((c % NCH) * CHUNK, CHUNK)]
        own.append(pltpu.make_async_copy(src, xg.at[c, 0], near.at[c]))
    for a, src in ((0, w_in), (1, w_out)):
        own.append(pltpu.make_async_copy(src, piece(a, z, None), near.at[2 * NCH + a]))
    for copy in own:
        copy.start()
    mg[0] = token_table(columns(routes[...]), columns(gates[...]), tiles[...])
    pl.semaphore_wait(barrier, len(others))

    def of_first(shape):
        return lax.rem(iota(shape, 0), ROWS) < ONE

    def pick(i, k):
        rows = dot(sel[k * ROWS : (k + 1) * ROWS, :], gathered(i)[...].reshape(ALL_TOK, -1), ((1,), (0,)))
        rows = rows.astype(BF16)
        if k == 0:
            arrived(i, 0)[...] = rows
        else:
            picked(i, k)[...] = rows
            across(i, k).start()

    def project(i):
        c, lo, hi = OUT[i]
        for k in range(1, NX):
            across(i, k).wait_recv()
        if c is None:
            return
        cols = slice(c % NCH * CHUNK + lo, c % NCH * CHUNK + hi)
        rows = rx[c, :, :, lo:hi].reshape(SEL, hi - lo)
        if c < NCH:
            values, total = [dot(rows, win[j, cols, :], ((1,), (0,))) for j in range(TILES_DEV)], hidden
        else:
            values, total = [dot(rows, wout[j, :, cols], ((1,), (1,))) for j in range(TILES_DEV)], back
        value = jnp.where(of_first((SEL, TILE)), values[0], values[1])
        if c % NCH == 0 and lo == 0:
            total[...] = value
        else:
            total[...] += value

    tasks = []
    for s in range(STARTS[-1] + HY + LAG + 1):
        for i in range(len(OUT)):
            if s == STARTS[i]:
                if OUT[i][0] is not None and OUT[i][1] == 0:
                    own[OUT[i][0]].wait()
                for way in range(2):
                    ring(i, 1, way).start()
        moving = [i for i in range(len(OUT)) if 1 <= s - STARTS[i] <= HY]
        late = [i for i in range(len(OUT)) if s - STARTS[i] == HY + LAG]
        for i in moving if s <= HY + 2 else reversed(moving):
            hop = s - STARTS[i]
            for way in range(2):
                ring(i, hop, way).wait_recv()
                if hop < HY:
                    ring(i, hop + 1, way).start()
            if hop == HY:
                if i == 0:
                    fill_selection(mg[...].reshape(ALL_TOK, 128), sel)
                tasks += [(pick, i, k) for k in (2, 1, 3, 0)]
            for task in [tasks.pop(0) for _ in range(min(2, len(tasks)))]:
                task[0](*task[1:])
        if s < 6 or s >= STARTS[-3] + HY:
            for task in tasks:
                task[0](*task[1:])
            tasks = []
        if s % 2 == 0 and s <= 2 * HZ:
            hop = s // 2
            for a in range(2):
                if hop == 0:
                    own[2 * NCH + a].wait()
                for way in range(2):
                    if hop > 0:
                        weights(a, hop, way).wait_recv()
                    if hop > 0 or way == 0:
                        twin(a, hop, way).start()
                    if hop < HZ:
                        weights(a, hop + 1, way).start()
        if s == 2 * HZ + 1:
            for a in range(2):
                for hop in range(HZ + 1):
                    for way in range(2 if hop > 0 else 1):
                        twin(a, hop, way).wait_recv()
        tasks += [(project, i) for i in late]

    for task in tasks:
        task[0](*task[1:])

    def term(i, k):
        c, lo, hi = BACK[i]
        return gp.at[k] if c is None else sx.at[c, k, :, lo:hi]

    def landed_terms(i):
        c, lo, hi = BACK[i]
        return bm if c is None else bx.at[c, :, :, lo:hi]

    def return_x(i, k):
        return send(term(i, k), landed_terms(i).at[k], qs.at[i, k], qr.at[i, k], at(y, x - k))

    def partial(i):
        c, lo, hi = BACK[i]
        return pm if c is None else xg.at[c, :, :, lo:hi]

    def outgoing(i, hop, way):
        c, lo, hi = BACK[i]
        return om.at[hop - 1, way] if c is None else xg.at[NCH + c, (hop - 1) * 2 + way, :, lo:hi]

    def incoming(i, hop, way):
        c, lo, hi = BACK[i]
        return im.at[hop - 1, way] if c is None else ib.at[c, hop - 1, way, :, lo:hi]

    def return_y(c, hop, way):
        src, dst = outgoing(c, hop, way), incoming(c, hop, way)
        if hop == 1:
            rows = pl.ds(way * HALF, HALF)
            src, dst = src.at[rows], dst.at[rows]
        return send(src, dst, rs.at[c, hop - 1, way], rr.at[c, hop - 1, way], at(y - 1 + 2 * way, x))

    def swap(a):
        src, dst = (parts_in, twin_in) if a == 0 else (parts_out, twin_out)
        return send(src.at[:, 1 - core], dst, ks.at[a], kr.at[a], at_z(z, 1 - core))

    def return_z(a, hop, way):
        src, dst = (zo_in, zi_in) if a == 0 else (zo_out, zi_out)
        src, dst = src.at[hop - 1, way], dst.at[hop - 1, way]
        if hop == 1:
            src, dst = src.at[pl.ds(way, 1)], dst.at[pl.ds(way, 1)]
        return send(src, dst, zs.at[a, hop - 1, way], zr.at[a, hop - 1, way], at_z(z - 1 + 2 * way, core))

    def chip_sum(a, slot, tile):
        home = lax.rem(z - slot + NZ, NZ)
        mine, other = (parts_in, twin_in) if a == 0 else (parts_out, twin_out)
        return mine[home, core, tile].astype(F32) + other[home, tile].astype(F32)

    lane = iota((SEL, 128), 1)
    tile = e * TILES_DEV + jnp.where(of_first((SEL, 128)), 0, 1)
    table = rm[...].reshape(SEL, 128).astype(F32)
    gate = jnp.sum(jnp.where(lane == TILES + tile, table, 0.0), axis=1, keepdims=True)
    act, slope = gelu_pair(hidden[...])
    gate_part = jnp.sum(act * back[...], axis=1, keepdims=True)
    terms = jnp.where(lane == tile, gate_part, 0.0).astype(BF16).reshape(NX, ROWS, 128)
    bm[0] = terms[0]
    for k in range(1, NX):
        gp[k] = terms[k]
    grad_hidden, gated_act = gate * back[...] * slope, gate * act
    first = of_first((SEL, TILE))
    for j in range(TILES_DEV):
        mine = first if j == 0 else jnp.logical_not(first)
        gh[j] = jnp.where(mine, grad_hidden, 0.0).astype(BF16)
        ga[j] = jnp.where(mine, gated_act, 0.0).astype(BF16)

    def set_out(i):
        c, lo, hi = BACK[i]
        if c is not None:
            cols = slice(c * CHUNK + lo, c * CHUNK + hi)
            rows = dot(gh[0], win[0, cols, :], ((1,), (1,))) + dot(gh[1], win[1, cols, :], ((1,), (1,)))
            rows = rows.astype(BF16).reshape(NX, ROWS, hi - lo)
            landed_terms(i)[0] = rows[0]
            for k in range(1, NX):
                term(i, k)[...] = rows[k]
        for k in (2, 1, 3):
            return_x(i, k).start()

    for i in range(len(OUT)):
        for k in range(1, NX):
            across(i, k).wait_send()
    for i in range(AHEAD):
        set_out(i)

    def tile_terms(a, c):
        rows = rx[a * NCH + c].reshape(SEL, CHUNK)
        for j in range(TILES_DEV):
            part = (dot(ga[j], rows, ((0,), (0,))) if a else dot(rows, gh[j], ((0,), (0,)))).astype(BF16)
            for i in range(CHUNK // SLICE):
                q = c * (CHUNK // SLICE) + i
                cols = slice(i * SLICE, (i + 1) * SLICE)
                if a:
                    parts_out[q // 2, q % 2, j] = part[:, cols]
                else:
                    parts_in[q // 2, q % 2, j] = part[cols, :]

    for a in range(2):
        for c in range(NCH):
            tile_terms(a, c)
        swap(a).start()
    for c in range(len(OUT)):
        for hop in range(1, HY + 1):
            for way in range(2):
                ring(c, hop, way).wait_send()

    for s in range(RETURNS[-1] + HY + 1):
        for c in range(len(BACK)):
            hop = s - RETURNS[c]
            if 1 <= hop < HY:
                for way in range(2):
                    return_y(c, hop, way).wait_recv()
                    slot = HY - hop if way == 0 else HY + hop
                    if hop == 1:
                        rows = slice(way * HALF, (way + 1) * HALF)
                        rest = slice((1 - way) * HALF, (2 - way) * HALF)
                        outgoing(c, 2, way)[rows] = (
                            partial(c)[slot, rows].astype(F32) + incoming(c, 1, way)[rows].astype(F32)
                        ).astype(BF16)
                        outgoing(c, 2, way)[rest] = partial(c)[slot, rest]
                    else:
                        outgoing(c, hop + 1, way)[...] = (
                            partial(c)[slot].astype(F32) + incoming(c, hop, way)[...].astype(F32)
                        ).astype(BF16)
                    return_y(c, hop + 1, way).start()
            if hop == HY:
                total = partial(c)[0].astype(F32)
                for way in range(2):
                    return_y(c, hop, way).wait_recv()
                    total += incoming(c, hop, way)[...].astype(F32)
                if BACK[c][0] is None:
                    of_tile = jnp.where(iota((TOK, 128), 1) < TILES, tile_experts(tiles[...]), -1.0)
                    cols = columns(routes[...])
                    ones = jnp.ones((8, 128), BF16)
                    for k in range(routes.shape[0]):
                        mine = jnp.where(cols[:, k : k + 1] == of_tile, total, 0.0).astype(BF16)
                        gg[k : k + 1, :] = dot(ones, mine, ((1,), (1,)))[0:1, :]
                else:
                    gt[:, BACK[c][0] * CHUNK + BACK[c][1] : BACK[c][0] * CHUNK + BACK[c][2]] = total.astype(BF16)
        for a in range(2):
            if s == 1:
                swap(a).wait_recv()
                for way in range(2):
                    (zo_in if a == 0 else zo_out)[0, way, way] = chip_sum(a, HZ, way).astype(BF16)
                    return_z(a, 1, way).start()
            hop = s - 1
            if 1 <= hop < HZ:
                stage, landed = (zo_in, zi_in) if a == 0 else (zo_out, zi_out)
                for way in range(2):
                    return_z(a, hop, way).wait_recv()
                    slot = HZ - hop if way == 0 else HZ + hop
                    for tile in range(TILES_DEV):
                        value = chip_sum(a, slot, tile)
                        if hop > 1 or tile == way:
                            value += landed[hop - 1, way, tile].astype(F32)
                        stage[hop, way, tile] = value.astype(BF16)
                    return_z(a, hop + 1, way).start()
            if hop == HZ:
                landed = zi_in if a == 0 else zi_out
                for way in range(2):
                    return_z(a, HZ, way).wait_recv()
                for tile in range(TILES_DEV):
                    value = chip_sum(a, 0, tile)
                    for way in range(2):
                        value += landed[HZ - 1, way, tile].astype(F32)
                    (gin if a == 0 else gout)[tile] = value
        if s in RETURNS:
            c = RETURNS.index(s)
            if c + AHEAD < len(BACK):
                set_out(c + AHEAD)
            for k in range(1, NX):
                return_x(c, k).wait_recv()
            rows = landed_terms(c)[...].reshape(SEL, -1)
            partial(c)[...] = dot(sel[...], rows, ((0,), (0,))).astype(BF16).reshape(NY, TOK, -1)
            for way in range(2):
                rows = slice(way * HALF, (way + 1) * HALF)
                outgoing(c, 1, way)[rows] = partial(c)[HY, rows]
                return_y(c, 1, way).start()

    for c in range(len(BACK)):
        for k in range(1, NX):
            return_x(c, k).wait_send()
        for hop in range(1, HY + 1):
            for way in range(2):
                return_y(c, hop, way).wait_send()
    for a in range(2):
        swap(a).wait_send()
        for hop in range(HZ + 1):
            for way in range(2):
                if hop > 0 or way == 0:
                    twin(a, hop, way).wait_send()
                if hop > 0:
                    weights(a, hop, way).wait_send()
                    return_z(a, hop, way).wait_send()


def layer(tokens, grad_out, routes, gates, tiles, w_in, w_out):
    vmem, anywhere = pl.BlockSpec(memory_space=pltpu.VMEM), pl.BlockSpec(memory_space=pl.ANY)
    dma = pltpu.SemaphoreType.DMA

    def hold(*shape):
        return pltpu.VMEM(shape, BF16)

    return pl.pallas_call(
        layer_kernel,
        out_shape=(
            jax.ShapeDtypeStruct((TOK, D), BF16),
            jax.ShapeDtypeStruct(routes.shape, F32),
            jax.ShapeDtypeStruct(w_in.shape, F32),
            jax.ShapeDtypeStruct(w_out.shape, F32),
        ),
        in_specs=[anywhere, anywhere, vmem, vmem, vmem, anywhere, anywhere],
        out_specs=(vmem,) * 4,
        scratch_shapes=[
            hold(2 * NCH, NY, TOK, CHUNK),
            hold(NY, TOK, 128),
            hold(2 * NCH, NX, ROWS, CHUNK),
            hold(NX, ROWS, 128),
            hold(2 * NCH, NX, ROWS, CHUNK),
            hold(NX, ROWS, 128),
            hold(SEL, ALL_TOK),
            hold(TILES_DEV, D, TILE),
            hold(TILES_DEV, TILE, D),
            pltpu.VMEM((SEL, TILE), F32),
            pltpu.VMEM((SEL, TILE), F32),
            hold(TILES_DEV, SEL, TILE),
            hold(TILES_DEV, SEL, TILE),
            hold(NX, ROWS, 128),
            hold(NCH, NX, ROWS, CHUNK),
            hold(NX, ROWS, 128),
            hold(NY, TOK, 128),
            hold(HY, 2, TOK, 128),
            hold(NCH, HY, 2, TOK, CHUNK),
            hold(HY, 2, TOK, 128),
            hold(NZ, 2, TILES_DEV, SLICE, TILE),
            hold(NZ, 2, TILES_DEV, TILE, SLICE),
            hold(NZ, TILES_DEV, SLICE, TILE),
            hold(NZ, TILES_DEV, TILE, SLICE),
            hold(HZ, 2, TILES_DEV, SLICE, TILE),
            hold(HZ, 2, TILES_DEV, SLICE, TILE),
            hold(HZ, 2, TILES_DEV, TILE, SLICE),
            hold(HZ, 2, TILES_DEV, TILE, SLICE),
            dma((2 * NCH + 2,)),
            dma((len(OUT), HY, 2)),
            dma((len(OUT), HY, 2)),
            dma((len(OUT), NX)),
            dma((len(OUT), NX)),
            dma((2, HZ, 2)),
            dma((2, HZ, 2)),
            dma((2, HZ + 1, 2)),
            dma((2, HZ + 1, 2)),
            dma((len(BACK), NX)),
            dma((len(BACK), NX)),
            dma((len(BACK), HY, 2)),
            dma((len(BACK), HY, 2)),
            dma((2,)),
            dma((2,)),
            dma((2, HZ, 2)),
            dma((2, HZ, 2)),
        ],
        compiler_params=pltpu.CompilerParams(
            collective_id=0, has_side_effects=True, vmem_limit_bytes=60 << 20
        ),
        name="layer",
    )(tokens, grad_out, routes, gates, tiles, w_in, w_out)


def finish_kernel(*refs):
    n = len(refs) // 2
    for i in range(n):
        refs[n + i][...] = refs[i][...]


def finish(*arrays):
    vmem = pl.BlockSpec(memory_space=pltpu.VMEM)
    return pl.pallas_call(
        finish_kernel,
        out_shape=tuple(jax.ShapeDtypeStruct(a.shape, a.dtype) for a in arrays),
        in_specs=[vmem] * len(arrays),
        out_specs=(vmem,) * len(arrays),
        name="finish",
    )(*arrays)


def on_device(tokens, grad_out, routes, gates, expert_tiles, w_in, w_out):
    results = layer(tokens, grad_out, routes.T, gates.T, expert_tiles.reshape(1, -1), w_in, w_out)
    grad_tokens, gates_rows, grad_in, grad_out_w = finish(*results)
    return grad_tokens, gates_rows.T, grad_in, grad_out_w


def solution(mesh):
    rows = P(("dp", "expert"), None)
    w_in, w_out = P("expert", "dp", None), P("expert", None, "dp")
    return jax.shard_map(
        on_device,
        mesh=mesh,
        in_specs=(rows, rows, rows, rows, P(), w_in, w_out),
        out_specs=(rows, rows, w_in, w_out),
        check_vma=False,
    )
```

```python
import jax
import jax.numpy as jnp
from jax import lax
from jax.experimental import pallas as pl
from jax.experimental.pallas import tpu as pltpu
from jax.sharding import PartitionSpec as P

MESH = pl.DeviceIdType.MESH
BF16, F32 = jnp.bfloat16, jnp.float32

NY, NX = 8, 4
TOK = 128
D, TILE = 2048, 256
TILES, TILES_DEV = 64, 2
MOST = 13
CHUNK = 512
NCH = D // CHUNK
ONE = 8 * MOST
ROWS = TILES_DEV * ONE
SEL = NX * ROWS
ALL_TOK = NY * TOK
NZ = 8
SLICE = D // (2 * NZ)
HALF = TOK // 2


def my_place():
    e, p = lax.axis_index("expert"), lax.axis_index("dp")
    return e // NX, e % NX, p // 2, p % 2


def at(y, x):
    return {"expert": lax.rem(y + NY, NY) * NX + lax.rem(x + NX, NX)}


def at_z(z, core):
    return {"dp": lax.rem(z + NZ, NZ) * 2 + core}


def partners():
    y, x, z, core = my_place()
    others = [at(y + 1, x), at(y - 1, x)] + [at(y, x + k) for k in range(1, NX)]
    others += [at_z(z + 1, core), at_z(z - 1, core), at_z(z, 1 - core)]
    return others


def dot(a, b, dims):
    return lax.dot_general(a, b, (dims, ((), ())), preferred_element_type=F32)


def send(src, dst, send_sem, recv_sem, to):
    return pltpu.make_async_remote_copy(
        src_ref=src, dst_ref=dst, send_sem=send_sem, recv_sem=recv_sem, device_id=to, device_id_type=MESH
    )


def iota(shape, dim):
    return lax.broadcasted_iota(jnp.int32, shape, dim)


def columns(rows):
    eye = jnp.where(iota((TOK, TOK), 0) == iota((TOK, TOK), 1), 1.0, 0.0).astype(BF16)
    return dot(eye, rows.astype(F32).astype(BF16), ((1,), (1,)))


def tile_experts(tiles):
    n = tiles.shape[1]
    upto = iota((n, n), 1) <= iota((n, n), 0)
    ends = jnp.sum(jnp.where(upto, tiles.astype(F32), 0.0), axis=1, keepdims=True)
    lane = iota((n, 128), 1) % TILES
    return jnp.sum(jnp.where(ends <= lane.astype(F32), 1.0, 0.0), axis=0, keepdims=True)


def token_table(routes, gates, tiles):
    of_tile = tile_experts(tiles)
    named = jnp.zeros((TOK, 128), F32)
    gate = jnp.zeros((TOK, 128), F32)
    for k in range(routes.shape[1]):
        hit = routes[:, k : k + 1] == of_tile
        named = jnp.where(hit, 1.0, named)
        gate = jnp.where(hit, gates[:, k : k + 1], gate)
    upto = iota((TOK, TOK), 1) <= iota((TOK, TOK), 0)
    rank = dot(jnp.where(upto, 1.0, 0.0).astype(BF16), named.astype(BF16), ((1,), (0,)))
    slot = jnp.where(named > 0.0, rank - 1.0, -1.0)
    return jnp.where(iota((TOK, 128), 1) < TILES, slot, gate).astype(BF16)


def fill_selection(table, sel):
    y, x, _, _ = my_place()
    a = iota((8, 128), 0)
    want = (y * NX + lax.rem(x + a // TILES_DEV, NX)) * TILES_DEV + a % TILES_DEV
    pick = jnp.where(iota((8, 128), 1) == want, 1.0, 0.0).astype(BF16)
    slots = dot(pick, table, ((1,), (1,)))
    source = iota((8, ALL_TOK), 1) // TOK
    place = jnp.where(slots >= 0.0, slots + (source * MOST).astype(F32), -1000.0)
    row = iota((ROWS, ALL_TOK), 0).astype(F32)
    for k in range(NX):
        first, second = place[2 * k : 2 * k + 1, :], place[2 * k + 1 : 2 * k + 2, :] + float(ONE)
        sel[k * ROWS : (k + 1) * ROWS, :] = jnp.where((first == row) | (second == row), 1.0, 0.0).astype(BF16)


def gelu_pair(v):
    t = jnp.tanh(0.7978845608 * (v + 0.044715 * v * v * v))
    act = 0.5 * v * (1.0 + t)
    slope = 0.5 * (1.0 + t) + 0.5 * v * (1.0 - t * t) * (0.7978845608 * (1.0 + 3.0 * 0.044715 * v * v))
    return act, slope


OUT = [(None, 0, 128), (0, 0, 256), (0, 256, 512)] + [(c, 0, CHUNK) for c in range(1, 2 * NCH - 1)]
OUT += [(2 * NCH - 1, 0, 256), (2 * NCH - 1, 256, 512)]
STARTS = [0, 0, 1, 2, 4, 6, 8, 10, 12, 14, 15]
LAG = 6
BACK = [(None, 0, 128)] + [(c, 0, CHUNK) for c in range(NCH)]
RETURNS = list(range(len(BACK)))
AHEAD = 2
HY, HZ = NY // 2, NZ // 2


def layer_kernel(
    tok, dy, routes, gates, tiles, w_in, w_out,
    gt, gg, gin, gout,
    xg, mg, sx, sm, rx, rm, sel, win, wout, hidden, back, gh, ga,
    gp, bx, bm, pm, om, ib, im, parts_in, parts_out, twin_in, twin_out, zo_in, zi_in, zo_out, zi_out,
    near, ys, yr, xs, xr, ws, wr, cs, cr, qs, qr, rs, rr, ks, kr, zs, zr,
):
    y, x, z, core = my_place()
    e = lax.axis_index("expert")

    def gathered(i):
        c, lo, hi = OUT[i]
        return mg if c is None else xg.at[c, :, :, lo:hi]

    def ring(c, hop, way):
        here = hop - 1 if way == 0 else (NY - (hop - 1)) % NY
        there = hop if way == 0 else NY - hop
        src, dst = gathered(c).at[here], gathered(c).at[there]
        if hop == HY:
            rows = pl.ds(way * HALF, HALF)
            src, dst = src.at[rows], dst.at[rows]
        return send(src, dst, ys.at[c, hop - 1, way], yr.at[c, hop - 1, way], at(y + 1 - 2 * way, x))

    def across(c, k):
        src, dst = picked(c, k), arrived(c, k)
        return send(src, dst, xs.at[c, k], xr.at[c, k], at(y, x + k))

    def picked(i, k):
        c, lo, hi = OUT[i]
        return sm.at[k] if c is None else sx.at[c, k, :, lo:hi]

    def arrived(i, k):
        c, lo, hi = OUT[i]
        return rm.at[k] if c is None else rx.at[c, k, :, lo:hi]

    def piece(a, home, tile):
        p = pl.multiple_of((lax.rem(home + 2 * NZ, NZ) * 2 + core) * SLICE, SLICE)
        j = slice(None) if tile is None else pl.ds(tile, 1)
        return win.at[j, pl.ds(p, SLICE), :] if a == 0 else wout.at[j, :, pl.ds(p, SLICE)]

    def weights(a, hop, way):
        part = piece(a, z - (hop - 1) * (1 - 2 * way), way if hop == HZ else None)
        return send(part, part, ws.at[a, hop - 1, way], wr.at[a, hop - 1, way], at_z(z + 1 - 2 * way, core))

    def twin(a, hop, way):
        part = piece(a, z - hop * (1 - 2 * way), way if hop == HZ else None)
        return send(part, part, cs.at[a, hop, way], cr.at[a, hop, way], at_z(z, 1 - core))

    barrier = pltpu.get_barrier_semaphore()
    others = partners()
    for other in others:
        pl.semaphore_signal(barrier, inc=1, device_id=other, device_id_type=MESH)

    own = []
    for c in range(2 * NCH):
        src = (tok if c < NCH else dy).at[:, pl.ds((c % NCH) * CHUNK, CHUNK)]
        own.append(pltpu.make_async_copy(src, xg.at[c, 0], near.at[c]))
    for a, src in ((0, w_in), (1, w_out)):
        own.append(pltpu.make_async_copy(src, piece(a, z, None), near.at[2 * NCH + a]))
    for copy in own:
        copy.start()
    mg[0] = token_table(columns(routes[...]), columns(gates[...]), tiles[...])
    pl.semaphore_wait(barrier, len(others))

    def of_first(shape):
        return lax.rem(iota(shape, 0), ROWS) < ONE

    def pick(i, k):
        rows = dot(sel[k * ROWS : (k + 1) * ROWS, :], gathered(i)[...].reshape(ALL_TOK, -1), ((1,), (0,)))
        rows = rows.astype(BF16)
        if k == 0:
            arrived(i, 0)[...] = rows
        else:
            picked(i, k)[...] = rows
            across(i, k).start()

    def project(i):
        c, lo, hi = OUT[i]
        for k in range(1, NX):
            across(i, k).wait_recv()
        if c is None:
            return
        cols = slice(c % NCH * CHUNK + lo, c % NCH * CHUNK + hi)
        rows = rx[c, :, :, lo:hi].reshape(SEL, hi - lo)
        if c < NCH:
            values, total = [dot(rows, win[j, cols, :], ((1,), (0,))) for j in range(TILES_DEV)], hidden
        else:
            values, total = [dot(rows, wout[j, :, cols], ((1,), (1,))) for j in range(TILES_DEV)], back
        value = jnp.where(of_first((SEL, TILE)), values[0], values[1])
        if c % NCH == 0 and lo == 0:
            total[...] = value
        else:
            total[...] += value

    tasks = []
    for s in range(STARTS[-1] + HY + LAG + 1):
        for i in range(len(OUT)):
            if s == STARTS[i]:
                if OUT[i][0] is not None and OUT[i][1] == 0:
                    own[OUT[i][0]].wait()
                for way in range(2):
                    ring(i, 1, way).start()
        moving = [i for i in range(len(OUT)) if 1 <= s - STARTS[i] <= HY]
        late = [i for i in range(len(OUT)) if s - STARTS[i] == HY + LAG]
        for i in moving if s <= HY + 2 else reversed(moving):
            hop = s - STARTS[i]
            for way in range(2):
                ring(i, hop, way).wait_recv()
                if hop < HY:
                    ring(i, hop + 1, way).start()
            if hop == HY:
                if i == 0:
                    fill_selection(mg[...].reshape(ALL_TOK, 128), sel)
                tasks += [(pick, i, k) for k in (2, 1, 3, 0)]
            for task in [tasks.pop(0) for _ in range(min(2, len(tasks)))]:
                task[0](*task[1:])
        if s < 6 or s >= STARTS[-3] + HY:
            for task in tasks:
                task[0](*task[1:])
            tasks = []
        if s % 2 == 0 and s <= 2 * HZ:
            hop = s // 2
            for a in range(2):
                if hop == 0:
                    own[2 * NCH + a].wait()
                for way in range(2):
                    if hop > 0:
                        weights(a, hop, way).wait_recv()
                    if hop > 0 or way == 0:
                        twin(a, hop, way).start()
                    if hop < HZ:
                        weights(a, hop + 1, way).start()
        if s == 2 * HZ + 1:
            for a in range(2):
                for hop in range(HZ + 1):
                    for way in range(2 if hop > 0 else 1):
                        twin(a, hop, way).wait_recv()
        tasks += [(project, i) for i in late]

    for task in tasks:
        task[0](*task[1:])

    def term(i, k):
        c, lo, hi = BACK[i]
        return gp.at[k] if c is None else sx.at[c, k, :, lo:hi]

    def landed_terms(i):
        c, lo, hi = BACK[i]
        return bm if c is None else bx.at[c, :, :, lo:hi]

    def return_x(i, k):
        return send(term(i, k), landed_terms(i).at[k], qs.at[i, k], qr.at[i, k], at(y, x - k))

    def partial(i):
        c, lo, hi = BACK[i]
        return pm if c is None else xg.at[c, :, :, lo:hi]

    def outgoing(i, hop, way):
        c, lo, hi = BACK[i]
        return om.at[hop - 1, way] if c is None else xg.at[NCH + c, (hop - 1) * 2 + way, :, lo:hi]

    def incoming(i, hop, way):
        c, lo, hi = BACK[i]
        return im.at[hop - 1, way] if c is None else ib.at[c, hop - 1, way, :, lo:hi]

    def return_y(c, hop, way):
        src, dst = outgoing(c, hop, way), incoming(c, hop, way)
        if hop == 1:
            rows = pl.ds(way * HALF, HALF)
            src, dst = src.at[rows], dst.at[rows]
        return send(src, dst, rs.at[c, hop - 1, way], rr.at[c, hop - 1, way], at(y - 1 + 2 * way, x))

    def swap(a):
        src, dst = (parts_in, twin_in) if a == 0 else (parts_out, twin_out)
        return send(src.at[:, 1 - core], dst, ks.at[a], kr.at[a], at_z(z, 1 - core))

    def return_z(a, hop, way):
        src, dst = (zo_in, zi_in) if a == 0 else (zo_out, zi_out)
        src, dst = src.at[hop - 1, way], dst.at[hop - 1, way]
        if hop == 1:
            src, dst = src.at[pl.ds(way, 1)], dst.at[pl.ds(way, 1)]
        return send(src, dst, zs.at[a, hop - 1, way], zr.at[a, hop - 1, way], at_z(z - 1 + 2 * way, core))

    def chip_sum(a, slot, tile):
        home = lax.rem(z - slot + NZ, NZ)
        mine, other = (parts_in, twin_in) if a == 0 else (parts_out, twin_out)
        return mine[home, core, tile].astype(F32) + other[home, tile].astype(F32)

    lane = iota((SEL, 128), 1)
    tile = e * TILES_DEV + jnp.where(of_first((SEL, 128)), 0, 1)
    table = rm[...].reshape(SEL, 128).astype(F32)
    gate = jnp.sum(jnp.where(lane == TILES + tile, table, 0.0), axis=1, keepdims=True)
    act, slope = gelu_pair(hidden[...])
    gate_part = jnp.sum(act * back[...], axis=1, keepdims=True)
    terms = jnp.where(lane == tile, gate_part, 0.0).astype(BF16).reshape(NX, ROWS, 128)
    bm[0] = terms[0]
    for k in range(1, NX):
        gp[k] = terms[k]
    grad_hidden, gated_act = gate * back[...] * slope, gate * act
    first = of_first((SEL, TILE))
    for j in range(TILES_DEV):
        mine = first if j == 0 else jnp.logical_not(first)
        gh[j] = jnp.where(mine, grad_hidden, 0.0).astype(BF16)
        ga[j] = jnp.where(mine, gated_act, 0.0).astype(BF16)

    def set_out(i):
        c, lo, hi = BACK[i]
        if c is not None:
            cols = slice(c * CHUNK + lo, c * CHUNK + hi)
            rows = dot(gh[0], win[0, cols, :], ((1,), (1,))) + dot(gh[1], win[1, cols, :], ((1,), (1,)))
            rows = rows.astype(BF16).reshape(NX, ROWS, hi - lo)
            landed_terms(i)[0] = rows[0]
            for k in range(1, NX):
                term(i, k)[...] = rows[k]
        for k in (2, 1, 3):
            return_x(i, k).start()

    for i in range(len(OUT)):
        for k in range(1, NX):
            across(i, k).wait_send()
    for i in range(AHEAD):
        set_out(i)

    def tile_terms(a, c):
        rows = rx[a * NCH + c].reshape(SEL, CHUNK)
        for j in range(TILES_DEV):
            part = (dot(ga[j], rows, ((0,), (0,))) if a else dot(rows, gh[j], ((0,), (0,)))).astype(BF16)
            for i in range(CHUNK // SLICE):
                q = c * (CHUNK // SLICE) + i
                cols = slice(i * SLICE, (i + 1) * SLICE)
                if a:
                    parts_out[q // 2, q % 2, j] = part[:, cols]
                else:
                    parts_in[q // 2, q % 2, j] = part[cols, :]

    for a in range(2):
        for c in range(NCH):
            tile_terms(a, c)
        swap(a).start()
    for c in range(len(OUT)):
        for hop in range(1, HY + 1):
            for way in range(2):
                ring(c, hop, way).wait_send()

    for s in range(RETURNS[-1] + HY + 1):
        for c in range(len(BACK)):
            hop = s - RETURNS[c]
            if 1 <= hop < HY:
                for way in range(2):
                    return_y(c, hop, way).wait_recv()
                    slot = HY - hop if way == 0 else HY + hop
                    if hop == 1:
                        rows = slice(way * HALF, (way + 1) * HALF)
                        rest = slice((1 - way) * HALF, (2 - way) * HALF)
                        outgoing(c, 2, way)[rows] = (
                            partial(c)[slot, rows].astype(F32) + incoming(c, 1, way)[rows].astype(F32)
                        ).astype(BF16)
                        outgoing(c, 2, way)[rest] = partial(c)[slot, rest]
                    else:
                        outgoing(c, hop + 1, way)[...] = (
                            partial(c)[slot].astype(F32) + incoming(c, hop, way)[...].astype(F32)
                        ).astype(BF16)
                    return_y(c, hop + 1, way).start()
            if hop == HY:
                total = partial(c)[0].astype(F32)
                for way in range(2):
                    return_y(c, hop, way).wait_recv()
                    total += incoming(c, hop, way)[...].astype(F32)
                if BACK[c][0] is None:
                    of_tile = jnp.where(iota((TOK, 128), 1) < TILES, tile_experts(tiles[...]), -1.0)
                    cols = columns(routes[...])
                    ones = jnp.ones((8, 128), BF16)
                    for k in range(routes.shape[0]):
                        mine = jnp.where(cols[:, k : k + 1] == of_tile, total, 0.0).astype(BF16)
                        gg[k : k + 1, :] = dot(ones, mine, ((1,), (1,)))[0:1, :]
                else:
                    gt[:, BACK[c][0] * CHUNK + BACK[c][1] : BACK[c][0] * CHUNK + BACK[c][2]] = total.astype(BF16)
        for a in range(2):
            if s == 1:
                swap(a).wait_recv()
                for way in range(2):
                    (zo_in if a == 0 else zo_out)[0, way, way] = chip_sum(a, HZ, way).astype(BF16)
                    return_z(a, 1, way).start()
            hop = s - 1
            if 1 <= hop < HZ:
                stage, landed = (zo_in, zi_in) if a == 0 else (zo_out, zi_out)
                for way in range(2):
                    return_z(a, hop, way).wait_recv()
                    slot = HZ - hop if way == 0 else HZ + hop
                    for tile in range(TILES_DEV):
                        value = chip_sum(a, slot, tile)
                        if hop > 1 or tile == way:
                            value += landed[hop - 1, way, tile].astype(F32)
                        stage[hop, way, tile] = value.astype(BF16)
                    return_z(a, hop + 1, way).start()
            if hop == HZ:
                landed = zi_in if a == 0 else zi_out
                for way in range(2):
                    return_z(a, HZ, way).wait_recv()
                for tile in range(TILES_DEV):
                    value = chip_sum(a, 0, tile)
                    for way in range(2):
                        value += landed[HZ - 1, way, tile].astype(F32)
                    (gin if a == 0 else gout)[tile] = value
        if s in RETURNS:
            c = RETURNS.index(s)
            if c + AHEAD < len(BACK):
                set_out(c + AHEAD)
            for k in range(1, NX):
                return_x(c, k).wait_recv()
            rows = landed_terms(c)[...].reshape(SEL, -1)
            partial(c)[...] = dot(sel[...], rows, ((0,), (0,))).astype(BF16).reshape(NY, TOK, -1)
            for way in range(2):
                rows = slice(way * HALF, (way + 1) * HALF)
                outgoing(c, 1, way)[rows] = partial(c)[HY, rows]
                return_y(c, 1, way).start()

    for c in range(len(BACK)):
        for k in range(1, NX):
            return_x(c, k).wait_send()
        for hop in range(1, HY + 1):
            for way in range(2):
                return_y(c, hop, way).wait_send()
    for a in range(2):
        swap(a).wait_send()
        for hop in range(HZ + 1):
            for way in range(2):
                if hop > 0 or way == 0:
                    twin(a, hop, way).wait_send()
                if hop > 0:
                    weights(a, hop, way).wait_send()
                    return_z(a, hop, way).wait_send()


def layer(tokens, grad_out, routes, gates, tiles, w_in, w_out):
    vmem, anywhere = pl.BlockSpec(memory_space=pltpu.VMEM), pl.BlockSpec(memory_space=pl.ANY)
    dma = pltpu.SemaphoreType.DMA

    def hold(*shape):
        return pltpu.VMEM(shape, BF16)

    return pl.pallas_call(
        layer_kernel,
        out_shape=(
            jax.ShapeDtypeStruct((TOK, D), BF16),
            jax.ShapeDtypeStruct(routes.shape, F32),
            jax.ShapeDtypeStruct(w_in.shape, F32),
            jax.ShapeDtypeStruct(w_out.shape, F32),
        ),
        in_specs=[anywhere, anywhere, vmem, vmem, vmem, anywhere, anywhere],
        out_specs=(vmem,) * 4,
        scratch_shapes=[
            hold(2 * NCH, NY, TOK, CHUNK),
            hold(NY, TOK, 128),
            hold(2 * NCH, NX, ROWS, CHUNK),
            hold(NX, ROWS, 128),
            hold(2 * NCH, NX, ROWS, CHUNK),
            hold(NX, ROWS, 128),
            hold(SEL, ALL_TOK),
            hold(TILES_DEV, D, TILE),
            hold(TILES_DEV, TILE, D),
            pltpu.VMEM((SEL, TILE), F32),
            pltpu.VMEM((SEL, TILE), F32),
            hold(TILES_DEV, SEL, TILE),
            hold(TILES_DEV, SEL, TILE),
            hold(NX, ROWS, 128),
            hold(NCH, NX, ROWS, CHUNK),
            hold(NX, ROWS, 128),
            hold(NY, TOK, 128),
            hold(HY, 2, TOK, 128),
            hold(NCH, HY, 2, TOK, CHUNK),
            hold(HY, 2, TOK, 128),
            hold(NZ, 2, TILES_DEV, SLICE, TILE),
            hold(NZ, 2, TILES_DEV, TILE, SLICE),
            hold(NZ, TILES_DEV, SLICE, TILE),
            hold(NZ, TILES_DEV, TILE, SLICE),
            hold(HZ, 2, TILES_DEV, SLICE, TILE),
            hold(HZ, 2, TILES_DEV, SLICE, TILE),
            hold(HZ, 2, TILES_DEV, TILE, SLICE),
            hold(HZ, 2, TILES_DEV, TILE, SLICE),
            dma((2 * NCH + 2,)),
            dma((len(OUT), HY, 2)),
            dma((len(OUT), HY, 2)),
            dma((len(OUT), NX)),
            dma((len(OUT), NX)),
            dma((2, HZ, 2)),
            dma((2, HZ, 2)),
            dma((2, HZ + 1, 2)),
            dma((2, HZ + 1, 2)),
            dma((len(BACK), NX)),
            dma((len(BACK), NX)),
            dma((len(BACK), HY, 2)),
            dma((len(BACK), HY, 2)),
            dma((2,)),
            dma((2,)),
            dma((2, HZ, 2)),
            dma((2, HZ, 2)),
        ],
        compiler_params=pltpu.CompilerParams(
            collective_id=0, has_side_effects=True, vmem_limit_bytes=60 << 20
        ),
        name="layer",
    )(tokens, grad_out, routes, gates, tiles, w_in, w_out)


def finish_kernel(*refs):
    n = len(refs) // 2
    for i in range(n):
        refs[n + i][...] = refs[i][...]


def finish(*arrays):
    vmem = pl.BlockSpec(memory_space=pltpu.VMEM)
    return pl.pallas_call(
        finish_kernel,
        out_shape=tuple(jax.ShapeDtypeStruct(a.shape, a.dtype) for a in arrays),
        in_specs=[vmem] * len(arrays),
        out_specs=(vmem,) * len(arrays),
        name="finish",
    )(*arrays)


def on_device(tokens, grad_out, routes, gates, expert_tiles, w_in, w_out):
    results = layer(tokens, grad_out, routes.T, gates.T, expert_tiles.reshape(1, -1), w_in, w_out)
    grad_tokens, gates_rows, grad_in, grad_out_w = finish(*results)
    return grad_tokens, gates_rows.T, grad_in, grad_out_w


def solution(mesh):
    rows = P(("dp", "expert"), None)
    w_in, w_out = P("expert", "dp", None), P("expert", None, "dp")
    return jax.shard_map(
        on_device,
        mesh=mesh,
        in_specs=(rows, rows, rows, rows, P(), w_in, w_out),
        out_specs=(rows, rows, w_in, w_out),
        check_vma=False,
    )
```
